512 devices in a mesh: ctx: 64 (over y, x, z_hi), ch: 8 (over z_lo, core).
Axes of the slice: x: 4, y: 8, z: 8 (z_hi: 2, z_lo: 4; z = z_hi * 4 + z_lo), core: 2. Of those that a mesh axis runs over, the one named last changes fastest.
Arguments:
- queries: bfloat16 [8192, 1024], P('ctx', 'ch'), may hold values from -5 to 5
- keys_in: bfloat16 [8192, 1024], P('ctx', 'ch'), may hold values from -5 to 5
- values: bfloat16 [8192, 1024], P('ctx', 'ch'), may hold values from -12 to 12
- hyena_query: bfloat16 [8192, 1024], P('ctx', 'ch'), may hold values from -3 to 3
- hyena_value: bfloat16 [8192, 1024], P('ctx', 'ch'), may hold values from -3 to 3
- filter_taps: bfloat16 [8192, 1024], P('ctx', 'ch'), may hold values from -6 to 6
- norm_gain: float32 [1024], P('ch'), may hold values from 0.5 to 1.5
- upstream: bfloat16 [8192, 1024], P('ctx', 'ch'), may hold values from -3 to 3
- block_order: int32 [128], replicated, may hold values from 0 to 127, each once
Outputs:
- grad_queries: bfloat16 [8192, 1024], P('ctx', 'ch')
- grad_keys: bfloat16 [8192, 1024], P('ctx', 'ch')
- grad_values: bfloat16 [8192, 1024], P('ctx', 'ch')
- grad_hyena_query: bfloat16 [8192, 1024], P('ctx', 'ch')
- grad_hyena_value: bfloat16 [8192, 1024], P('ctx', 'ch')
- grad_taps: bfloat16 [8192, 1024], P('ctx', 'ch')
The draws below stay inside these ranges and needn't reach their ends.
Inputs may be any that keep to these rules, and one draw needn't show every extreme that they name: block_order[j] is the sequence block of 64 positions that stored rows j * 64 to (j + 1) * 64 - 1 hold; each block once.
All inputs are finite; a program needn't handle non-finite values.
Results may differ from the reference program's by a relative error of at most 0.039.
Values may be sent and summed in bfloat16 or wider, within the bound.
A program may use at most 64 MiB of HBM per device.

```python
import math
import jax
import jax.numpy as jnp
from jax import lax

HEAD_DIM = 128
HALF = 64
SEQ = 8192
WIDTH = 1024
N_CTX = 64


def draw_queries(key, part):
    key = jax.random.fold_in(key, 1)
    return jnp.clip(jax.random.normal(key, (SEQ, WIDTH)), -4.0, 4.0).astype(jnp.bfloat16)


def draw_keys_in(key, part):
    key = jax.random.fold_in(key, 2)
    return jnp.clip(jax.random.normal(key, (SEQ, WIDTH)), -4.0, 4.0).astype(jnp.bfloat16)


def draw_values(key, part):
    key = jax.random.fold_in(key, 3)
    columns = 3.0 ** (jnp.arange(WIDTH) / (WIDTH - 1.0))
    return (jnp.clip(jax.random.normal(key, (SEQ, WIDTH)), -4.0, 4.0) * columns).astype(jnp.bfloat16)


def shard_levels(key, dims, shards, smallest, top_value):
    def one(axis_at, blocks):
        draws = jax.random.uniform(jax.random.fold_in(jax.random.fold_in(key, 6), axis_at), (blocks,), jnp.float32, smallest / len(shards), top_value / len(shards))
        return jnp.repeat(jnp.exp(draws), dims[axis_at] // blocks).reshape((-1,) + (1,) * (len(dims) - axis_at - 1))

    loudness = one(*shards[0])
    for cut in shards[1:]:
        loudness = loudness * one(*cut)
    return loudness


def centred(own_key, shape, scale, most, cuts=(), kind=jnp.bfloat16):
    gain = shard_levels(own_key, shape, cuts, -0.22, 0.18) if cuts else 1.0
    result = jax.random.normal(own_key, shape, jnp.float32) * scale * gain
    return jnp.minimum(jnp.maximum(result, -most), most).astype(kind)


def setup_inputs(seed: int = 0) -> dict:
    key_list = jax.random.split(jax.random.key(seed), 10)
    queries = draw_queries(jax.random.fold_in(key_list[9], 71), 0)
    keys_in = draw_keys_in(jax.random.fold_in(key_list[9], 71), 0)
    values = draw_values(jax.random.fold_in(key_list[9], 71), 0)
    hyena_query = centred(key_list[3], (SEQ, WIDTH), 0.6, 3.0, ((0, 64), (1, 8)))
    hyena_value = centred(key_list[4], (SEQ, WIDTH), 0.6, 3.0, ((0, 64), (1, 8)))
    filter_taps = centred(key_list[5], (SEQ, WIDTH), 1.0, 6.0, ((0, 64), (1, 8)))
    norm_gain = jnp.clip(1.0 + 0.1 * jax.random.normal(key_list[6], (WIDTH,), jnp.float32), 0.5, 1.5)
    upstream = centred(key_list[7], (SEQ, WIDTH), 0.6, 3.0, ((0, 64), (1, 8)))
    block_order = jax.random.permutation(key_list[8], 2 * N_CTX).astype(jnp.int32)
    return dict(queries=queries, keys_in=keys_in, values=values, hyena_query=hyena_query, hyena_value=hyena_value, filter_taps=filter_taps, norm_gain=norm_gain, upstream=upstream, block_order=block_order)


HIGHEST = lax.Precision.HIGHEST

def rounded(value):
    return lax.optimization_barrier(value.astype(jnp.bfloat16)).astype(jnp.float32)

def matmul(left, right):
    return jnp.dot(left, right, precision=HIGHEST)

def split_heads(field):
    return field.astype(jnp.float32).reshape(SEQ, WIDTH // HEAD_DIM, HEAD_DIM).transpose(1, 0, 2)

def join_heads(field):
    return field.transpose(1, 0, 2).reshape(SEQ, WIDTH)

def reference(queries, keys_in, values, hyena_query, hyena_value, filter_taps, norm_gain, upstream, block_order):
    rows = jnp.arange(SEQ, dtype=jnp.int32)
    positions = block_order[rows // HALF] * HALF + rows % HALF
    scale = 1.0 / math.sqrt(HEAD_DIM)
    block = min(SEQ, 1024)
    starts = jnp.arange(SEQ // block, dtype=jnp.int32) * block

    def forward_head(operands):
        query_head, key_head, value_head = operands

        def one_block(start):
            query_block = lax.dynamic_slice_in_dim(query_head, start, block, 0)
            block_pos = lax.dynamic_slice_in_dim(positions, start, block, 0)
            scores = matmul(query_block, key_head.T) * scale
            visible = positions[None, :] <= block_pos[:, None]
            scores = jnp.where(visible, scores, -jnp.inf)
            peak = lax.optimization_barrier(jnp.max(scores, axis=1, keepdims=True))
            weights = jnp.exp(scores - peak)
            total = lax.optimization_barrier(jnp.sum(weights, axis=1, keepdims=True))
            output = matmul(rounded(weights), value_head) / total
            return (output, (peak + jnp.log(total))[:, 0])
        output, lse = lax.map(one_block, starts)
        return (output.reshape(SEQ, HEAD_DIM), lse.reshape(SEQ))

    def backward_head(operands):
        query_head, key_head, value_head, dout_head, lse_head, delta_head = operands

        def one_block(carry, start):
            grad_key, grad_value = carry
            query_block = lax.dynamic_slice_in_dim(query_head, start, block, 0)
            dout_block = lax.dynamic_slice_in_dim(dout_head, start, block, 0)
            lse_block = lax.dynamic_slice_in_dim(lse_head, start, block, 0)
            delta_block = lax.dynamic_slice_in_dim(delta_head, start, block, 0)
            block_pos = lax.dynamic_slice_in_dim(positions, start, block, 0)
            scores = matmul(query_block, key_head.T) * scale
            visible = positions[None, :] <= block_pos[:, None]
            probs = jnp.exp(jnp.where(visible, scores - lse_block[:, None], -jnp.inf))
            dprobs = matmul(dout_block, value_head.T)
            dscores = probs * (dprobs - delta_block[:, None])
            probs_low = rounded(probs)
            dscores_low = rounded(dscores)
            grad_value = grad_value + matmul(probs_low.T, dout_block)
            grad_key = grad_key + matmul(dscores_low.T, query_block) * scale
            grad_query = matmul(dscores_low, key_head) * scale
            return ((grad_key, grad_value), grad_query)
        empty = jnp.zeros((SEQ, HEAD_DIM), jnp.float32)
        (grad_key, grad_value), grad_query = lax.scan(one_block, (empty, empty), starts)
        return (grad_query.reshape(SEQ, HEAD_DIM), grad_key, grad_value)
    query_split = split_heads(queries)
    key_split = split_heads(keys_in)
    value_split = split_heads(values)
    attended, lse = lax.map(forward_head, (query_split, key_split, value_split))
    attended = join_heads(attended).astype(jnp.bfloat16)
    act = attended.astype(jnp.float32)
    mean_square = lax.optimization_barrier(jnp.sum(act * act, axis=1, keepdims=True)) / WIDTH
    inv_root = lax.rsqrt(mean_square + 1e-06)
    normed = act * inv_root * norm_gain
    mixed = (normed * hyena_value.astype(jnp.float32)).astype(jnp.bfloat16)
    gated = (upstream.astype(jnp.float32) * hyena_query.astype(jnp.float32)).astype(jnp.bfloat16)
    count = 2 * N_CTX
    inverse = jnp.zeros((count,), jnp.int32).at[block_order].set(jnp.arange(count, dtype=jnp.int32))

    def to_true(field):
        return field.reshape(count, HALF, WIDTH)[inverse].reshape(SEQ, WIDTH)

    def to_stored(field):
        return field.reshape(count, HALF, WIDTH)[block_order].reshape(SEQ, WIDTH)
    length = 2 * SEQ
    taps = filter_taps.astype(jnp.float32) * SEQ ** (-0.5)
    spec_taps = jnp.fft.rfft(taps, n=length, axis=0)
    spec_mixed = jnp.fft.rfft(to_true(mixed).astype(jnp.float32), n=length, axis=0)
    spec_gated = jnp.fft.rfft(to_true(gated).astype(jnp.float32), n=length, axis=0)
    conv = jnp.fft.irfft(spec_taps * spec_mixed, n=length, axis=0)[:SEQ]
    back_mixed = jnp.fft.irfft(jnp.conj(spec_taps) * spec_gated, n=length, axis=0)[:SEQ]
    back_taps = jnp.fft.irfft(jnp.conj(spec_mixed) * spec_gated, n=length, axis=0)[:SEQ]
    conv = to_stored(conv).astype(jnp.bfloat16)
    back_mixed = to_stored(back_mixed).astype(jnp.bfloat16)
    grad_taps = (back_taps * SEQ ** (-0.5)).astype(jnp.bfloat16)
    grad_hyena_query = (upstream.astype(jnp.float32) * conv.astype(jnp.float32)).astype(jnp.bfloat16)
    back_wide = back_mixed.astype(jnp.float32)
    grad_hyena_value = (back_wide * normed).astype(jnp.bfloat16)
    scaled = back_wide * hyena_value.astype(jnp.float32) * norm_gain
    inner = lax.optimization_barrier(jnp.sum(scaled * act, axis=1, keepdims=True))
    grad_attended = (inv_root * scaled - act * inv_root ** 3 * (inner / WIDTH)).astype(jnp.bfloat16)
    dout_split = split_heads(grad_attended)
    delta = lax.optimization_barrier(jnp.sum(dout_split * split_heads(attended), axis=2))
    grad_query, grad_key, grad_value = lax.map(backward_head, (query_split, key_split, value_split, dout_split, lse, delta))
    return (join_heads(grad_query).astype(jnp.bfloat16), join_heads(grad_key).astype(jnp.bfloat16), join_heads(grad_value).astype(jnp.bfloat16), grad_hyena_query, grad_hyena_value, grad_taps)
```

```python
import math

import jax
import jax.numpy as jnp
from jax import lax
from jax.experimental import pallas as pl
from jax.experimental.pallas import tpu as pltpu
from jax.sharding import PartitionSpec as P

T = 128
HALF = 64
N = 8
SEQ = T * N * N
WIDTH = 1024
LOG2E = 1.4426950408889634
HIDDEN = -1e30
MESH = pl.DeviceIdType.MESH
F32 = jnp.float32
BF16 = jnp.bfloat16


def nn(a, b):
    return lax.dot_general(a, b, (((1,), (0,)), ((), ())), preferred_element_type=F32)


def nt(a, b):
    return lax.dot_general(a, b, (((1,), (1,)), ((), ())), preferred_element_type=F32)


def iota(shape, dim):
    return lax.broadcasted_iota(jnp.int32, shape, dim)


def one_hot(cond):
    return jnp.where(cond, 1.0, 0.0).astype(BF16)


def flip(x):
    return x.astype(F32).T


def row_source(r):
    return (r & 7) * N + (r >> 4)


def row_channel(r):
    return (r >> 3) & 1


def to_rows():
    out, inn = iota((T, T), 0), iota((T, T), 1)
    return one_hot(inn == (out & 7) * 16 + (out >> 4) * 2 + ((out >> 3) & 1))


def from_rows():
    inn, out = iota((T, T), 1), iota((T, T), 0)
    return one_hot(out == (inn & 7) * 16 + (inn >> 4) * 2 + ((inn >> 3) & 1))


def toeplitz(chunks, table, first):
    ahead = iota((HALF, T), 1) >= iota((HALF, T), 0)

    def step(n, before):
        line = jnp.broadcast_to(chunks[pl.ds(n, 1), :], (HALF, T))
        now = pltpu.roll(line, 0, 1, stride=1, stride_axis=0)
        table[pl.ds(first, HALF), pl.ds(pl.multiple_of(n * T, T), T)] = jnp.where(
            ahead, now, before
        ).astype(BF16)
        return now

    lax.fori_loop(0, SEQ // T, step, jnp.zeros((HALF, T), F32), unroll=4)


def long_product(table, rows, blocks):
    lane = iota((HALF, T), 1)

    def step(g, total):
        parts = []
        for u in range(4):
            d = g * 4 + u
            moved = pltpu.roll(blocks, d, 1)
            parts.append(jnp.where(lane >= d, moved, 0.0).astype(BF16))
        right = jnp.concatenate(parts, axis=0)
        left = table[pl.ds(0, rows), pl.ds(pl.multiple_of(g * 256, 256), 256)]
        return total + nn(left, right)

    return lax.fori_loop(0, T // 4, step, jnp.zeros((rows, T), F32), unroll=4)


def kernel(
    order_s, order_v, q_ref, k_ref, v_ref, hq_ref, hv_ref, taps_ref, gain_ref, up_ref,
    dq_out, dk_out, dv_out, dhq_out, dhv_out, dtaps_out,
    q_all, k_all, v_all, vt, kt, scores,
    tg1_s, tg1, tg2_s, tg2, o_s, o_r, os_s, os_r, bm1_s, bm1, bm2_s, bm2,
    st_s, st_r, do_s, do_r, ds_s, ds_r, mx1_s, mx1, mx2_s, mx2,
    cg1_s, cg1, cg2_s, cg2, dq_s, dq_r, dkv_s, dkv_r,
    up_t, hv_t, hvg_t, gain_t, table, chunks, dk_acc, dv_acc,
    send, recv,
):
    me = lax.axis_index("ctx")
    head = lax.axis_index("ch")
    y = lax.div(me, N)
    c = lax.rem(me, N)
    scale = 1.0 / math.sqrt(T)
    tap_scale = SEQ ** (-0.5)

    def y_peer(k):
        p = lax.rem(y + k, N)
        return p, (p * N + c, head)

    def c_peer(k):
        p = lax.rem(c + k, N)
        return p, (y * N + p, head)

    def h_peer(k):
        p = lax.rem(head + k, N)
        return p, (me, p)

    def spread(peer, src, dst, slot, sem):
        def step(k, _):
            p, device = peer(k)
            pltpu.make_async_remote_copy(
                src_ref=src(p),
                dst_ref=dst.at[slot],
                send_sem=send.at[sem],
                recv_sem=recv.at[sem],
                device_id=device,
                device_id_type=MESH,
            ).start()
            return 0

        lax.fori_loop(1, N, step, 0)

    def arrived(dst, sem):
        part = dst.at[pl.ds(0, N - 1)]
        pltpu.make_async_copy(part, part, recv.at[sem]).wait()

    def left(dst, sem):
        part = dst.at[pl.ds(0, N - 1)]
        pltpu.make_async_copy(part, part, send.at[sem]).wait()

    barrier = pltpu.get_barrier_semaphore()

    def greet(k, _):
        for peer in (y_peer, c_peer, h_peer):
            pl.semaphore_signal(barrier, inc=1, device_id=peer(k)[1], device_id_type=MESH)
        return 0

    lax.fori_loop(1, N, greet, 0)

    up = up_ref[...].astype(F32)
    gated = (up * hq_ref[...].astype(F32)).astype(BF16)
    tg1_s[:, 0:16, :] = flip(gated).astype(BF16).reshape(N, 16, T)
    tg1_s[:, 16:32, :] = flip(taps_ref[...]).astype(BF16).reshape(N, 16, T)
    tg1[y] = tg1_s[y]
    q_all[y] = q_ref[...]
    k_all[c] = k_ref[...]
    v_all[c] = v_ref[...]
    pl.semaphore_wait(barrier, 3 * (N - 1))

    spread(y_peer, lambda p: tg1_s.at[p], tg1, y, 0)
    spread(c_peer, lambda p: k_ref, k_all, c, 1)
    spread(y_peer, lambda p: q_ref, q_all, y, 2)
    spread(c_peer, lambda p: v_ref, v_all, c, 3)

    up_t[...] = flip(up)
    hv_t[...] = flip(hv_ref[...])
    gain_t[...] = jnp.broadcast_to(gain_ref[...], (T, T)).T
    hvg_t[...] = hv_t[...] * gain_t[...]

    row = iota((T, T), 1)
    line = iota((T, T), 0)
    order = jnp.broadcast_to(order_v[...].astype(F32), (8, T)).astype(BF16)
    place = [
        nn(order, one_hot(line == row_source(row) * 2 + h))[0:1, :].astype(jnp.int32) for h in (0, 1)
    ]
    ours = [row_channel(row) == j for j in (0, 1)]

    def forward(j, h):
        return one_hot(ours[j] & (place[h] == line))

    def backward(j, h):
        return one_hot(ours[j] & (place[h] == T - 1 - line))

    def lag_order(j, h):
        return one_hot(ours[j] & (row_source(row) * 2 + h == T - 1 - line))

    arrived(tg1, 0)
    order_in = to_rows()
    for lo in (0, 16):
        tg2_s[:, lo : lo + 16, :] = (
            nn(order_in, tg1[:, lo : lo + 16, :].reshape(T, T)).astype(BF16).reshape(N, 16, T)
        )
    tg2[c] = tg2_s[c]
    spread(c_peer, lambda p: tg2_s.at[p], tg2, c, 4)
    arrived(tg2, 4)

    grads = tg2[:, 0:16, :].reshape(T, T)
    taps = tg2[:, 16:32, :].reshape(T, T)
    grads_t = flip(grads).astype(BF16)
    narrow_row, narrow_line = iota((HALF, T), 1), iota((HALF, T), 0)
    back_t = [jnp.zeros((HALF, T), F32)] * 2
    for j in (0, 1):
        mine = row_channel(narrow_row) == j
        chunks[j] = nn(one_hot(mine & (row_source(narrow_row) == narrow_line)), taps)
        toeplitz(chunks.at[j], table.at[j], 0)
        blocks = nt(grads_t[0:HALF], backward(j, 0)) + nt(grads_t[HALF:T], backward(j, 1))
        result = (long_product(table.at[j], HALF, blocks) * tap_scale).astype(BF16)
        for h in (0, 1):
            back_t[h] = back_t[h] + nn(result, backward(j, h))
    bm1_s[...] = flip(jnp.concatenate(back_t, axis=0)).astype(BF16).reshape(N, 16, T)
    bm1[c] = bm1_s[c]
    spread(c_peer, lambda p: bm1_s.at[p], bm1, c, 5)

    arrived(k_all, 1)
    arrived(q_all, 2)
    arrived(v_all, 3)
    for i in range(N):
        vt[:, i * T : (i + 1) * T] = flip(v_all[i]).astype(BF16)
        kt[:, i * T : (i + 1) * T] = flip(k_all[i]).astype(BF16)

    within = iota((1, 2 * T), 1)
    deep = iota((HALF, 2 * T), 0)

    def query_places(pair):
        base = within & (HALF - 1)
        spot = jnp.zeros((1, 2 * T), jnp.int32)
        for e in range(4):
            block = order_s[((pair * 2 + e // 2) * N + c) * 2 + e % 2]
            spot = jnp.where((within >> 6) == e, block * HALF, spot)
        return spot + base

    def masked(tile, pair_q, spots):
        keys = k_all[2 * tile : 2 * tile + 2].reshape(2 * T, T)
        raw = nt(keys, pair_q) * (scale * LOG2E)
        out = []
        for e in range(4):
            block = order_s[y * 16 + tile * 4 + e]
            out.append(
                jnp.where(deep <= spots - block * HALF, raw[e * HALF : (e + 1) * HALF], HIDDEN)
            )
        return jnp.concatenate(out, axis=0)

    def attend(pair, _):
        pair_q = q_all[pl.ds(pair * 2, 2)].reshape(2 * T, T)
        spots = query_places(pair)
        peak = jnp.full((1, 2 * T), HIDDEN, F32)
        for tile in range(4):
            part = masked(tile, pair_q, spots)
            scores[tile * 256 : (tile + 1) * 256, :] = part
            peak = jnp.maximum(peak, jnp.max(part, axis=0, keepdims=True))
        total = jnp.zeros((1, 2 * T), F32)
        out = jnp.zeros((T, 2 * T), F32)
        for tile in range(4):
            weights = jnp.exp2(scores[tile * 256 : (tile + 1) * 256, :] - peak)
            total = total + jnp.sum(weights, axis=0, keepdims=True)
            out = out + nn(vt[:, tile * 256 : (tile + 1) * 256], weights.astype(BF16))
        for e in (0, 1):
            lanes = slice(e * T, (e + 1) * T)
            o_s[pair * 2 + e] = out[:, lanes].astype(BF16)
            os_s[pair * 2 + e] = jnp.concatenate([peak[:, lanes], total[:, lanes]], axis=0)
        return 0

    lax.fori_loop(0, 4, attend, 0)
    o_r[y] = o_s[y]
    os_r[y] = os_s[y]
    spread(y_peer, lambda p: os_s.at[p], os_r, y, 6)
    spread(y_peer, lambda p: o_s.at[p], o_r, y, 7)

    arrived(bm1, 5)
    order_out = from_rows()
    bm2_s[...] = nn(order_out, bm1[...].reshape(T, T)).astype(BF16).reshape(N, 16, T)
    bm2[y] = bm2_s[y]
    spread(y_peer, lambda p: bm2_s.at[p], bm2, y, 8)

    for j in (0, 1):
        mine = row_channel(narrow_row) == j
        flat = jnp.zeros((HALF, T), F32)
        for h in (0, 1):
            for hh in (0, 1):
                turn = one_hot(
                    ((row >> 6) == hh) & (line == h * HALF + HALF - 1 - (row & (HALF - 1)))
                )
                pick = one_hot(mine & (place[h] == T - 1 - 2 * narrow_line - hh))
                flat = flat + nn(pick, nn(grads, turn).astype(BF16))
        chunks[j] = flat
        toeplitz(chunks.at[j], table.at[j], HALF)

    arrived(os_r, 6)
    arrived(o_r, 7)
    peak = os_r[0, 0:1, :]
    for i in range(1, N):
        peak = jnp.maximum(peak, os_r[i, 0:1, :])
    total = jnp.zeros((1, T), F32)
    mix = jnp.zeros((T, T), F32)
    for i in range(N):
        factor = jnp.exp2(os_r[i, 0:1, :] - peak)
        total = total + factor * os_r[i, 1:2, :]
        mix = mix + factor * o_r[i].astype(F32)
    lse = peak + jnp.log2(total)
    act = (mix / total).astype(BF16).astype(F32)
    arrived(bm2, 8)
    back = bm2[...].reshape(T, T).astype(F32)
    scaled = back * hvg_t[...]
    st_s[...] = jnp.concatenate(
        [jnp.sum(act * act, axis=0, keepdims=True), jnp.sum(scaled * act, axis=0, keepdims=True)],
        axis=0,
    )
    st_r[head] = st_s[...]
    spread(h_peer, lambda p: st_s, st_r, head, 9)
    arrived(st_r, 9)
    sums = st_r[0]
    for i in range(1, N):
        sums = sums + st_r[i]
    inv_root = lax.rsqrt(sums[0:1, :] / WIDTH + 1e-06)
    inner = sums[1:2, :]
    grad_att = (inv_root * scaled - act * (inv_root * inv_root * inv_root) * (inner / WIDTH)).astype(BF16)
    do_s[...] = grad_att
    do_r[y] = grad_att
    spread(y_peer, lambda p: do_s, do_r, y, 10)
    delta = jnp.sum(grad_att.astype(F32) * act, axis=0, keepdims=True)
    ds_s[...] = jnp.concatenate([lse, delta], axis=0)
    ds_r[y] = ds_s[...]
    spread(y_peer, lambda p: ds_s, ds_r, y, 11)
    normed = act * inv_root * gain_t[...]
    mx1_s[...] = (normed * hv_t[...]).astype(BF16).reshape(N, 16, T)
    mx1[y] = mx1_s[y]
    spread(y_peer, lambda p: mx1_s.at[p], mx1, y, 12)
    dhv_out[...] = flip((back * normed).astype(BF16)).astype(BF16)

    arrived(mx1, 12)
    mx2_s[...] = nn(order_in, mx1[...].reshape(T, T)).astype(BF16).reshape(N, 16, T)
    mx2[c] = mx2_s[c]
    spread(c_peer, lambda p: mx2_s.at[p], mx2, c, 13)

    dk_acc[...] = jnp.zeros((N * T, T), F32)
    dv_acc[...] = jnp.zeros((N * T, T), F32)
    arrived(do_r, 10)
    arrived(ds_r, 11)

    def grad(pair, _):
        pair_q = q_all[pl.ds(pair * 2, 2)].reshape(2 * T, T)
        spots = query_places(pair)
        low, high = do_r[pair * 2], do_r[pair * 2 + 1]
        pair_do = jnp.concatenate([low, high], axis=1)
        both = jnp.concatenate([ds_r[pair * 2], ds_r[pair * 2 + 1]], axis=1)
        dq = jnp.zeros((T, 2 * T), F32)
        for tile in range(4):
            rows = slice(tile * 256, (tile + 1) * 256)
            probs = jnp.exp2(masked(tile, pair_q, spots) - both[0:1, :])
            dprobs = nn(v_all[2 * tile : 2 * tile + 2].reshape(2 * T, T), pair_do)
            dscores = (probs * (dprobs - both[1:2, :])).astype(BF16)
            dv_acc[rows, :] += nt(probs.astype(BF16), pair_do)
            dk_acc[rows, :] += nn(dscores, pair_q)
            dq = dq + nn(kt[:, rows], dscores)
        for e in (0, 1):
            dq_s[pair * 2 + e] = (dq[:, e * T : (e + 1) * T] * scale).astype(BF16)
        return 0

    lax.fori_loop(0, 4, grad, 0)
    dkv_s[:, 0:T, :] = (dk_acc[...] * scale).astype(BF16).reshape(N, T, T)
    dkv_s[:, T : 2 * T, :] = dv_acc[...].astype(BF16).reshape(N, T, T)
    spread(c_peer, lambda p: dkv_s.at[p], dkv_r, c, 14)
    dkv_r[c] = dkv_s[c]
    spread(y_peer, lambda p: dq_s.at[p], dq_r, y, 15)
    dq_r[y] = dq_s[y]

    arrived(mx2, 13)
    within_half = one_hot(line == (row >> 6) * HALF + HALF - 1 - (row & (HALF - 1)))
    turned_t = flip(nn(mx2[...].reshape(T, T), within_half)).astype(BF16)
    conv_t = [jnp.zeros((HALF, T), F32)] * 2
    lags_t = [jnp.zeros((HALF, T), F32)] * 2
    for j in (0, 1):
        blocks = nt(turned_t[0:HALF], forward(j, 0)) + nt(turned_t[HALF:T], forward(j, 1))
        result = (long_product(table.at[j], T, blocks) * tap_scale).astype(BF16)
        for h in (0, 1):
            conv_t[h] = conv_t[h] + nn(result[0:HALF], forward(j, h))
            lags_t[h] = lags_t[h] + nn(result[HALF:T], lag_order(j, h))
    conv_rows = nn(flip(jnp.concatenate(conv_t, axis=0)).astype(BF16), within_half)
    cg1_s[:, 0:16, :] = conv_rows.astype(BF16).reshape(N, 16, T)
    cg1_s[:, 16:32, :] = flip(jnp.concatenate(lags_t, axis=0)).astype(BF16).reshape(N, 16, T)
    cg1[c] = cg1_s[c]
    spread(c_peer, lambda p: cg1_s.at[p], cg1, c, 16)
    arrived(cg1, 16)
    for lo in (0, 16):
        cg2_s[:, lo : lo + 16, :] = (
            nn(order_out, cg1[:, lo : lo + 16, :].reshape(T, T)).astype(BF16).reshape(N, 16, T)
        )
    cg2[y] = cg2_s[y]
    spread(y_peer, lambda p: cg2_s.at[p], cg2, y, 17)

    arrived(dq_r, 15)
    grad_q = dq_r[0].astype(F32)
    for i in range(1, N):
        grad_q = grad_q + dq_r[i].astype(F32)
    dq_out[...] = grad_q.T.astype(BF16)
    arrived(dkv_r, 14)
    grad_kv = dkv_r[0].astype(F32)
    for i in range(1, N):
        grad_kv = grad_kv + dkv_r[i].astype(F32)
    dk_out[...] = grad_kv[0:T].astype(BF16)
    dv_out[...] = grad_kv[T : 2 * T].astype(BF16)

    arrived(cg2, 17)
    dhq_out[...] = flip(up_t[...] * cg2[:, 0:16, :].reshape(T, T).astype(F32)).astype(BF16)
    dtaps_out[...] = flip(cg2[:, 16:32, :].reshape(T, T)).astype(BF16)

    for sem, dst in enumerate(
        (tg1, k_all, q_all, v_all, tg2, bm1, os_r, o_r, bm2, st_r, do_r, ds_r, mx1, mx2, dkv_r, dq_r, cg1, cg2)
    ):
        left(dst, sem)


def per_device(queries, keys_in, values, hq, hv, taps, gain, upstream, order):
    def vmem(*shape, dtype=BF16):
        return pltpu.VMEM(shape, dtype)

    pair16 = vmem(N, 16, T)
    pair32 = vmem(N, 32, T)
    square = vmem(N, T, T)
    tall = vmem(N, 2 * T, T)
    lines = vmem(N, 2, T, dtype=F32)
    wide = vmem(T, T, dtype=F32)
    in_vmem = pl.BlockSpec(memory_space=pltpu.VMEM)
    out = jax.ShapeDtypeStruct((T, T), BF16)
    return pl.pallas_call(
        kernel,
        out_shape=(out,) * 6,
        in_specs=[pl.BlockSpec(memory_space=pltpu.SMEM)] + [in_vmem] * 9,
        out_specs=(in_vmem,) * 6,
        scratch_shapes=[
            square, square, square, vmem(T, N * T), vmem(T, N * T), vmem(N * T, 2 * T, dtype=F32),
            pair32, pair32, pair32, pair32, square, square, lines, lines, pair16, pair16, pair16, pair16,
            vmem(2, T, dtype=F32), lines, vmem(T, T), square, vmem(2, T, dtype=F32), lines,
            pair16, pair16, pair16, pair16,
            pair32, pair32, pair32, pair32, square, square, tall, tall,
            wide, wide, wide, wide, vmem(2, T, SEQ), vmem(2, HALF, T, dtype=F32),
            vmem(N * T, T, dtype=F32), vmem(N * T, T, dtype=F32),
            pltpu.SemaphoreType.DMA((18,)), pltpu.SemaphoreType.DMA((18,)),
        ],
        compiler_params=pltpu.CompilerParams(
            collective_id=0, has_side_effects=True, vmem_limit_bytes=48 * 1024 * 1024
        ),
        name="pair_backward",
    )(order, order.reshape(1, -1), queries, keys_in, values, hq, hv, taps, gain.reshape(1, -1), upstream)


def solution(mesh):
    rows = P("ctx", "ch")
    return jax.shard_map(
        per_device,
        mesh=mesh,
        in_specs=(rows,) * 6 + (P("ch"), rows, P()),
        out_specs=(rows,) * 6,
        check_vma=False,
    )
```

```python
import math

import jax
import jax.numpy as jnp
from jax import lax
from jax.experimental import pallas as pl
from jax.experimental.pallas import tpu as pltpu
from jax.sharding import PartitionSpec as P

T = 128
HALF = 64
N = 8
SEQ = T * N * N
WIDTH = 1024
LOG2E = 1.4426950408889634
HIDDEN = -1e30
MESH = pl.DeviceIdType.MESH
F32 = jnp.float32
BF16 = jnp.bfloat16


def nn(a, b):
    return lax.dot_general(a, b, (((1,), (0,)), ((), ())), preferred_element_type=F32)


def nt(a, b):
    return lax.dot_general(a, b, (((1,), (1,)), ((), ())), preferred_element_type=F32)


def iota(shape, dim):
    return lax.broadcasted_iota(jnp.int32, shape, dim)


def one_hot(cond):
    return jnp.where(cond, 1.0, 0.0).astype(BF16)


def flip(x):
    return x.astype(F32).T


def row_source(r):
    return (r & 7) * N + (r >> 4)


def row_channel(r):
    return (r >> 3) & 1


def to_rows():
    out, inn = iota((T, T), 0), iota((T, T), 1)
    return one_hot(inn == (out & 7) * 16 + (out >> 4) * 2 + ((out >> 3) & 1))


def from_rows():
    inn, out = iota((T, T), 1), iota((T, T), 0)
    return one_hot(out == (inn & 7) * 16 + (inn >> 4) * 2 + ((inn >> 3) & 1))


def toeplitz(chunks, table, first):
    ahead = iota((HALF, T), 1) >= iota((HALF, T), 0)

    def step(n, before):
        after = []
        for j in (0, 1):
            line = jnp.broadcast_to(chunks[j, pl.ds(n, 1), :], (HALF, T))
            now = pltpu.roll(line, 0, 1, stride=1, stride_axis=0)
            table[j, pl.ds(first, HALF), pl.ds(pl.multiple_of(n * T, T), T)] = jnp.where(
                ahead, now, before[j]
            ).astype(BF16)
            after.append(now)
        return tuple(after)

    empty = jnp.zeros((HALF, T), F32)
    lax.fori_loop(0, SEQ // T, step, (empty, empty), unroll=4)


def long_products(table, steps, wide):
    totals = [jnp.zeros((T, wide), F32)] * 2
    for part in range(4):
        top = part * 32
        rows = T - top

        def step(g, sums):
            p = part * 8 + g
            out = []
            for j in (0, 1):
                pair = [
                    steps[j, pl.ds(T + top - 4 * p - 2 * u, rows), :].astype(BF16) for u in (0, 1)
                ]
                right = table[j, 0:wide, pl.ds(pl.multiple_of(p * 256, 256), 256)]
                out.append(sums[j] + nt(jnp.concatenate(pair, axis=1), right))
            return tuple(out)

        sums = lax.fori_loop(0, 8, step, tuple(t[top:] for t in totals), unroll=2)
        if top:
            sums = [jnp.concatenate([totals[j][0:top], sums[j]], axis=0) for j in (0, 1)]
        totals = list(sums)
    return totals


def kernel(
    order_h, q_h, k_h, v_h, hq_h, hv_h, taps_h, gain_h, up_h,
    packed,
    order_s, order_v, hq_ref, hv_ref, taps_ref, gain_ref, up_ref,
    q_all, k_all, v_all, vt, kt, scores,
    tg1_s, tg1, tg2_s, tg2, o_s, o_r, os_s, os_r, bm1_s, bm1, bm2_s, bm2,
    ss_s, ss_r, in_s, in_r, do_s, do_r, ds_s, ds_r, mx1_s, mx1, mx2_s, mx2,
    cg1_s, cg1, cg2_s, cg2, dq_s, dq_r, dkv_s, dkv_r,
    up_t, hv_t, hvg_t, gain_t, table, chunks, steps, dk_acc, dv_acc,
    send, recv, load,
):
    me = lax.axis_index("ctx")
    head = lax.axis_index("ch")
    y = lax.div(me, N)
    c = lax.rem(me, N)
    scale = 1.0 / math.sqrt(T)
    tap_scale = SEQ ** (-0.5)

    def y_peer(k):
        p = lax.rem(y + k, N)
        return p, (p * N + c, head)

    def c_peer(k):
        p = lax.rem(c + k, N)
        return p, (y * N + p, head)

    def h_peer(k):
        p = lax.rem(head + k, N)
        return p, (me, p)

    started = []

    def spread(peer, src, dst, slot):
        sem = len(started)
        started.append(dst)

        def step(k, _):
            p, device = peer(k)
            pltpu.make_async_remote_copy(
                src_ref=src(p),
                dst_ref=dst.at[slot],
                send_sem=send.at[sem],
                recv_sem=recv.at[sem],
                device_id=device,
                device_id_type=MESH,
            ).start()
            return 0

        lax.fori_loop(1, N, step, 0)

        def arrived():
            part = dst.at[pl.ds(0, N - 1)]
            pltpu.make_async_copy(part, part, recv.at[sem]).wait()

        return arrived

    barrier = pltpu.get_barrier_semaphore()

    def greet(k, _):
        for peer in (y_peer, c_peer, h_peer):
            pl.semaphore_signal(barrier, inc=1, device_id=peer(k)[1], device_id_type=MESH)
        return 0

    lax.fori_loop(1, N, greet, 0)

    loads = [
        pltpu.make_async_copy(src, dst, load.at[i])
        for i, (src, dst) in enumerate(
            (
                (up_h, up_ref), (hq_h, hq_ref), (taps_h, taps_ref), (q_h, q_all.at[y]), (k_h, k_all.at[c]),
                (v_h, v_all.at[c]), (hv_h, hv_ref), (gain_h, gain_ref), (order_h, order_s), (order_h, order_v),
            )
        )
    ]
    for each in loads:
        each.start()
    for each in loads[0:3]:
        each.wait()
    up = up_ref[...].astype(F32)
    gated = (up * hq_ref[...].astype(F32)).astype(BF16)
    tg1_s[:, 0:16, :] = flip(gated).astype(BF16).reshape(N, 16, T)
    tg1_s[:, 16:32, :] = flip(taps_ref[...]).astype(BF16).reshape(N, 16, T)
    tg1[y] = tg1_s[y]
    for each in loads[3:]:
        each.wait()
    pl.semaphore_wait(barrier, 3 * (N - 1))

    tg1_here = spread(y_peer, lambda p: tg1_s.at[p], tg1, y)
    k_here = spread(c_peer, lambda p: k_all.at[c], k_all, c)
    q_here = spread(y_peer, lambda p: q_all.at[y], q_all, y)
    v_here = spread(c_peer, lambda p: v_all.at[c], v_all, c)

    up_t[...] = flip(up)
    hv_t[...] = flip(hv_ref[...])
    gain_t[...] = jnp.broadcast_to(gain_ref[...], (T, T)).T
    hvg_t[...] = hv_t[...] * gain_t[...]
    steps[:, 0:T, :] = jnp.zeros((2, T, T), F32)
    dk_acc[...] = jnp.zeros((N * T, T), F32)
    dv_acc[...] = jnp.zeros((N * T, T), F32)

    lane = iota((T, T), 1)
    line = iota((T, T), 0)
    order = jnp.broadcast_to(order_v[...].astype(F32), (8, T)).astype(BF16)
    place_f = [nn(order, one_hot(line == row_source(lane) * 2 + h))[0:1, :] for h in (0, 1)]
    place = [p.astype(jnp.int32) for p in place_f]
    place_t = [jnp.broadcast_to(p, (T, T)).T.astype(jnp.int32) for p in place_f]
    ours = [row_channel(lane) == j for j in (0, 1)]
    ours_t = [row_channel(line) == j for j in (0, 1)]
    here = lane & (HALF - 1)

    def lay_out(rows, turned, reverse):
        moved = [
            nn(rows, one_hot((line == h * HALF + (HALF - 1 - here if turned else here)) & ((lane >> 6) == e))).astype(BF16)
            for h in (0, 1)
            for e in (0, 1)
        ]
        for j in (0, 1):
            total = jnp.zeros((T, T), F32)
            for h in (0, 1):
                for e in (0, 1):
                    want = T - 1 - line + e if reverse else line - e
                    total = total + nn(one_hot(ours[j] & (place[h] == want)), moved[h * 2 + e])
            steps[j, T : 2 * T, :] = total

    def collect(results, spot, first, turned):
        total = jnp.zeros((T, T), F32)
        for h in (0, 1):
            mine = jnp.zeros((T, results[0].shape[1]), F32)
            for j in (0, 1):
                mine = mine + nn(one_hot(ours_t[j] & (spot[h] == lane)), results[j])
            wide = results[0].shape[1]
            a, b = iota((wide, T), 0), iota((wide, T), 1)
            inside = b & (HALF - 1)
            put = (a == first + (HALF - 1 - inside if turned else inside)) & ((b >> 6) == h)
            total = total + nn(mine.astype(BF16), one_hot(put))
        return total.astype(BF16)

    within = iota((1, 2 * T), 1)
    deep = iota((HALF, 2 * T), 0)

    def query_places(pair):
        base = within & (HALF - 1)
        spot = jnp.zeros((1, 2 * T), jnp.int32)
        for e in range(4):
            block = order_s[0, ((pair * 2 + e // 2) * N + c) * 2 + e % 2]
            spot = jnp.where((within >> 6) == e, block * HALF, spot)
        return spot + base

    def masked(tile, pair_q, spots):
        keys = k_all[2 * tile : 2 * tile + 2].reshape(2 * T, T)
        raw = nt(keys, pair_q) * (scale * LOG2E)
        out = []
        for e in range(4):
            block = order_s[0, y * 16 + tile * 4 + e]
            out.append(
                jnp.where(deep <= spots - block * HALF, raw[e * HALF : (e + 1) * HALF], HIDDEN)
            )
        return jnp.concatenate(out, axis=0)

    def attend(pair, _):
        pair_q = q_all[pl.ds(pair * 2, 2)].reshape(2 * T, T)
        spots = query_places(pair)
        peak = jnp.full((1, 2 * T), HIDDEN, F32)
        for tile in range(4):
            part = masked(tile, pair_q, spots)
            scores[tile * 256 : (tile + 1) * 256, :] = part
            peak = jnp.maximum(peak, jnp.max(part, axis=0, keepdims=True))
        total = jnp.zeros((1, 2 * T), F32)
        out = jnp.zeros((T, 2 * T), F32)
        for tile in range(4):
            weights = jnp.exp2(scores[tile * 256 : (tile + 1) * 256, :] - peak)
            total = total + jnp.sum(weights, axis=0, keepdims=True)
            out = out + nn(vt[:, tile * 256 : (tile + 1) * 256], weights.astype(BF16))
        for e in (0, 1):
            lanes = slice(e * T, (e + 1) * T)
            o_s[pair * 2 + e] = out[:, lanes].astype(BF16)
            os_s[pair * 2 + e] = jnp.concatenate([peak[:, lanes], total[:, lanes]], axis=0)
        return 0

    def forward_part():
        k_here()
        q_here()
        v_here()
        for i in range(N):
            vt[:, i * T : (i + 1) * T] = flip(v_all[i]).astype(BF16)
            kt[:, i * T : (i + 1) * T] = flip(k_all[i]).astype(BF16)
        lax.fori_loop(0, 4, attend, 0)
        o_r[y] = o_s[y]
        os_r[y] = os_s[y]
        os_here = spread(y_peer, lambda p: os_s.at[p], os_r, y)
        o_here = spread(y_peer, lambda p: o_s.at[p], o_r, y)
        return os_here, o_here

    tg1_here()
    order_in = to_rows()
    order_out = from_rows()
    for lo in (0, 16):
        tg2_s[:, lo : lo + 16, :] = (
            nn(order_in, tg1[:, lo : lo + 16, :].reshape(T, T)).astype(BF16).reshape(N, 16, T)
        )
    tg2[c] = tg2_s[c]
    tg2_here = spread(c_peer, lambda p: tg2_s.at[p], tg2, c)

    os_here, o_here = forward_part()

    tg2_here()
    grads = tg2[:, 0:16, :].reshape(T, T)
    taps = tg2[:, 16:32, :].reshape(T, T)
    narrow_lane, narrow_line = iota((HALF, T), 1), iota((HALF, T), 0)
    narrow_ours = [row_channel(narrow_lane) == j for j in (0, 1)]
    for j in (0, 1):
        chunks[j] = nn(one_hot(narrow_ours[j] & (row_source(narrow_lane) == narrow_line)), taps)
    toeplitz(chunks, table, 0)
    lay_out(grads, False, True)
    backs = [(r * tap_scale).astype(BF16) for r in long_products(table, steps, HALF)]
    flipped_t = [T - 1 - p for p in place_t]
    bm1_s[...] = collect(backs, flipped_t, 0, False).reshape(N, 16, T)
    bm1[c] = bm1_s[c]
    bm1_here = spread(c_peer, lambda p: bm1_s.at[p], bm1, c)

    flats = [jnp.zeros((HALF, T), F32)] * 2
    for h in (0, 1):
        for hh in (0, 1):
            turn = one_hot(((lane >> 6) == hh) & (line == h * HALF + HALF - 1 - here))
            turned = nn(grads, turn).astype(BF16)
            for j in (0, 1):
                pick = one_hot(narrow_ours[j] & (place[h] == T - 1 - 2 * narrow_line - hh))
                flats[j] = flats[j] + nn(pick, turned)
    for j in (0, 1):
        chunks[j] = flats[j]
    toeplitz(chunks, table, HALF)

    os_here()
    o_here()
    peak = os_r[0, 0:1, :]
    for i in range(1, N):
        peak = jnp.maximum(peak, os_r[i, 0:1, :])
    total = jnp.zeros((1, T), F32)
    mix = jnp.zeros((T, T), F32)
    for i in range(N):
        factor = jnp.exp2(os_r[i, 0:1, :] - peak)
        total = total + factor * os_r[i, 1:2, :]
        mix = mix + factor * o_r[i].astype(F32)
    lse = peak + jnp.log2(total)
    act = (mix / total).astype(BF16).astype(F32)
    ss_s[...] = jnp.sum(act * act, axis=0, keepdims=True)
    ss_r[head] = ss_s[...]
    ss_here = spread(h_peer, lambda p: ss_s, ss_r, head)

    bm1_here()
    bm2_s[...] = nn(order_out, bm1[...].reshape(T, T)).astype(BF16).reshape(N, 16, T)
    bm2[y] = bm2_s[y]
    bm2_here = spread(y_peer, lambda p: bm2_s.at[p], bm2, y)

    ss_here()
    square = ss_r[0]
    for i in range(1, N):
        square = square + ss_r[i]
    inv_root = lax.rsqrt(square / WIDTH + 1e-06)
    normed = act * inv_root * gain_t[...]
    mx1_s[...] = (normed * hv_t[...]).astype(BF16).reshape(N, 16, T)
    mx1[y] = mx1_s[y]
    mx1_here = spread(y_peer, lambda p: mx1_s.at[p], mx1, y)

    bm2_here()
    back = bm2[...].reshape(T, T).astype(F32)
    scaled = back * hvg_t[...]
    in_s[...] = jnp.sum(scaled * act, axis=0, keepdims=True)
    in_r[head] = in_s[...]
    in_here = spread(h_peer, lambda p: in_s, in_r, head)
    packed[4] = flip((back * normed).astype(BF16)).astype(BF16)

    mx1_here()
    mx2_s[...] = nn(order_in, mx1[...].reshape(T, T)).astype(BF16).reshape(N, 16, T)
    mx2[c] = mx2_s[c]
    mx2_here = spread(c_peer, lambda p: mx2_s.at[p], mx2, c)

    in_here()
    inner = in_r[0]
    for i in range(1, N):
        inner = inner + in_r[i]
    grad_att = (
        inv_root * scaled - act * (inv_root * inv_root * inv_root) * (inner / WIDTH)
    ).astype(BF16)
    do_s[...] = grad_att
    do_r[y] = grad_att
    do_here = spread(y_peer, lambda p: do_s, do_r, y)
    delta = jnp.sum(grad_att.astype(F32) * act, axis=0, keepdims=True)
    ds_s[...] = jnp.concatenate([lse, delta], axis=0)
    ds_r[y] = ds_s[...]
    ds_here = spread(y_peer, lambda p: ds_s, ds_r, y)

    mx2_here()
    lay_out(mx2[...].reshape(T, T), True, False)
    lates = [(r * tap_scale).astype(BF16) for r in long_products(table, steps, T)]
    lag_t = [T - 1 - (row_source(line) * 2 + h) for h in (0, 1)]
    cg1_s[:, 0:16, :] = collect(lates, place_t, 0, True).reshape(N, 16, T)
    cg1_s[:, 16:32, :] = collect(lates, lag_t, HALF, False).reshape(N, 16, T)
    cg1[c] = cg1_s[c]
    cg1_here = spread(c_peer, lambda p: cg1_s.at[p], cg1, c)

    do_here()
    ds_here()

    def grad(pair, _):
        pair_q = q_all[pl.ds(pair * 2, 2)].reshape(2 * T, T)
        spots = query_places(pair)
        low, high = do_r[pair * 2], do_r[pair * 2 + 1]
        pair_do = jnp.concatenate([low, high], axis=1)
        both = jnp.concatenate([ds_r[pair * 2], ds_r[pair * 2 + 1]], axis=1)
        dq = jnp.zeros((T, 2 * T), F32)
        for tile in range(4):
            rows = slice(tile * 256, (tile + 1) * 256)
            probs = jnp.exp2(masked(tile, pair_q, spots) - both[0:1, :])
            dprobs = nn(v_all[2 * tile : 2 * tile + 2].reshape(2 * T, T), pair_do)
            dscores = (probs * (dprobs - both[1:2, :])).astype(BF16)
            dv_acc[rows, :] += nt(probs.astype(BF16), pair_do)
            dk_acc[rows, :] += nn(dscores, pair_q)
            dq = dq + nn(kt[:, rows], dscores)
        for e in (0, 1):
            dq_s[pair * 2 + e] = (dq[:, e * T : (e + 1) * T] * scale).astype(BF16)
        return 0

    lax.fori_loop(0, 4, grad, 0)
    dkv_s[:, 0:T, :] = (dk_acc[...] * scale).astype(BF16).reshape(N, T, T)
    dkv_s[:, T : 2 * T, :] = dv_acc[...].astype(BF16).reshape(N, T, T)
    dkv_here = spread(c_peer, lambda p: dkv_s.at[p], dkv_r, c)
    dkv_r[c] = dkv_s[c]
    dq_here = spread(y_peer, lambda p: dq_s.at[p], dq_r, y)
    dq_r[y] = dq_s[y]

    cg1_here()
    for lo in (0, 16):
        cg2_s[:, lo : lo + 16, :] = (
            nn(order_out, cg1[:, lo : lo + 16, :].reshape(T, T)).astype(BF16).reshape(N, 16, T)
        )
    cg2[y] = cg2_s[y]
    cg2_here = spread(y_peer, lambda p: cg2_s.at[p], cg2, y)

    dq_here()
    grad_q = dq_r[0].astype(F32)
    for i in range(1, N):
        grad_q = grad_q + dq_r[i].astype(F32)
    packed[0] = grad_q.T.astype(BF16)
    dkv_here()
    grad_kv = dkv_r[0].astype(F32)
    for i in range(1, N):
        grad_kv = grad_kv + dkv_r[i].astype(F32)
    packed[1] = grad_kv[0:T].astype(BF16)
    packed[2] = grad_kv[T : 2 * T].astype(BF16)

    cg2_here()
    packed[3] = flip(up_t[...] * cg2[:, 0:16, :].reshape(T, T).astype(F32)).astype(BF16)
    packed[5] = flip(cg2[:, 16:32, :].reshape(T, T)).astype(BF16)

    for sem, dst in enumerate(started):
        part = dst.at[pl.ds(0, N - 1)]
        pltpu.make_async_copy(part, part, send.at[sem]).wait()


def unpack(packed, *rest):
    outs, done = rest[:-1], rest[-1]
    moves = [pltpu.make_async_copy(packed.at[i], out, done.at[i]) for i, out in enumerate(outs)]
    for move in moves:
        move.start()
    for move in moves:
        move.wait()


def per_device(queries, keys_in, values, hq, hv, taps, gain, upstream, order):
    def vmem(*shape, dtype=BF16):
        return pltpu.VMEM(shape, dtype)

    pair16 = vmem(N, 16, T)
    pair32 = vmem(N, 32, T)
    square = vmem(N, T, T)
    tall = vmem(N, 2 * T, T)
    lines = vmem(N, 2, T, dtype=F32)
    wide = vmem(T, T, dtype=F32)
    one = vmem(T, T)
    in_hbm = pl.BlockSpec(memory_space=pltpu.HBM)
    packed = pl.pallas_call(
        kernel,
        out_shape=jax.ShapeDtypeStruct((6, T, T), BF16),
        in_specs=[in_hbm] * 9,
        out_specs=pl.BlockSpec(memory_space=pltpu.VMEM),
        scratch_shapes=[
            pltpu.SMEM((1, T), jnp.int32), vmem(1, T, dtype=jnp.int32), one, one, one, vmem(1, T, dtype=F32), one,
            square, square, square, vmem(T, N * T), vmem(T, N * T), vmem(N * T, 2 * T, dtype=F32),
            pair32, pair32, pair32, pair32, square, square, lines, lines, pair16, pair16, pair16, pair16,
            vmem(1, T, dtype=F32), vmem(N, 1, T, dtype=F32), vmem(1, T, dtype=F32), vmem(N, 1, T, dtype=F32),
            one, square, vmem(2, T, dtype=F32), lines, pair16, pair16, pair16, pair16,
            pair32, pair32, pair32, pair32, square, square, tall, tall,
            wide, wide, wide, wide, vmem(2, T, SEQ), vmem(2, HALF, T, dtype=F32), vmem(2, 2 * T, T, dtype=F32),
            vmem(N * T, T, dtype=F32), vmem(N * T, T, dtype=F32),
            pltpu.SemaphoreType.DMA((20,)), pltpu.SemaphoreType.DMA((20,)), pltpu.SemaphoreType.DMA((10,)),
        ],
        compiler_params=pltpu.CompilerParams(
            collective_id=0, has_side_effects=True, vmem_limit_bytes=60 * 1024 * 1024
        ),
        name="pair_backward",
    )(order.reshape(1, -1), queries, keys_in, values, hq, hv, taps, gain.reshape(1, -1), upstream)
    return pl.pallas_call(
        unpack,
        out_shape=(jax.ShapeDtypeStruct((T, T), BF16),) * 6,
        in_specs=[in_hbm],
        out_specs=(in_hbm,) * 6,
        scratch_shapes=[pltpu.SemaphoreType.DMA((6,))],
        compiler_params=pltpu.CompilerParams(vmem_limit_bytes=60 * 1024 * 1024),
        name="unpack",
    )(packed)


def solution(mesh):
    rows = P("ctx", "ch")
    return jax.shard_map(
        per_device,
        mesh=mesh,
        in_specs=(rows,) * 6 + (P("ch"), rows, P()),
        out_specs=(rows,) * 6,
        check_vma=False,
    )
```

```python
import math

import jax
import jax.numpy as jnp
from jax import lax
from jax.experimental import pallas as pl
from jax.experimental.pallas import tpu as pltpu
from jax.sharding import PartitionSpec as P

T = 128
HALF = 64
N = 8
SEQ = T * N * N
WIDTH = 1024
LOG2E = 1.4426950408889634
HIDDEN = -1e30
MESH = pl.DeviceIdType.MESH
F32 = jnp.float32
BF16 = jnp.bfloat16


def nn(a, b):
    return lax.dot_general(a, b, (((1,), (0,)), ((), ())), preferred_element_type=F32)


def nt(a, b):
    return lax.dot_general(a, b, (((1,), (1,)), ((), ())), preferred_element_type=F32)


def iota(shape, dim):
    return lax.broadcasted_iota(jnp.int32, shape, dim)


def one_hot(cond):
    return jnp.where(cond, 1.0, 0.0).astype(BF16)


def flip(x):
    return x.astype(F32).T


def row_source(r):
    return r >> 1


def row_channel(r):
    return r & 1


def interleave(first, second):
    out, inn = iota((2 * T, T), 0), iota((2 * T, T), 1)
    return sum(
        nn(one_hot(out == (inn >> 1) * 4 + 2 * k + (inn & 1)), field) for k, field in enumerate((first, second))
    ).astype(BF16)


def separate(rows, k):
    out, inn = iota((T, 2 * T), 0), iota((T, 2 * T), 1)
    return nn(one_hot(inn == (out >> 1) * 4 + 2 * k + (out & 1)), rows).astype(BF16)


def toeplitz(chunks, table, first):
    ahead = iota((HALF, T), 1) >= iota((HALF, T), 0)

    def step(n, before):
        after = []
        for j in (0, 1):
            line = jnp.broadcast_to(chunks[j, pl.ds(n, 1), :], (HALF, T))
            now = pltpu.roll(line, 0, 1, stride=1, stride_axis=0)
            table[j, pl.ds(first, HALF), pl.ds(pl.multiple_of(n * T, T), T)] = jnp.where(
                ahead, now, before[j]
            ).astype(BF16)
            after.append(now)
        return tuple(after)

    empty = jnp.zeros((HALF, T), F32)
    lax.fori_loop(0, SEQ // T, step, (empty, empty), unroll=4)


def long_products(table, steps, wide):
    totals = [jnp.zeros((T, wide), F32)] * 2
    for part in range(4):
        top = part * 32
        rows = T - top

        def step(g, sums):
            p = part * 8 + g
            out = []
            for j in (0, 1):
                pair = [
                    steps[j, pl.ds(T + top - 4 * p - 2 * u, rows), :].astype(BF16) for u in (0, 1)
                ]
                right = table[j, 0:wide, pl.ds(pl.multiple_of(p * 256, 256), 256)]
                out.append(sums[j] + nt(jnp.concatenate(pair, axis=1), right))
            return tuple(out)

        sums = lax.fori_loop(0, 8, step, tuple(t[top:] for t in totals), unroll=2)
        if top:
            sums = [jnp.concatenate([totals[j][0:top], sums[j]], axis=0) for j in (0, 1)]
        totals = list(sums)
    return totals


def kernel(
    order_h, q_h, k_h, v_h, hq_h, hv_h, taps_h, gain_h, up_h,
    packed,
    order_s, order_v, hq_ref, hv_ref, taps_ref, gain_ref, up_ref,
    q_all, k_all, v_all, vt, kt, scores,
    tg_s, tg, o_s, o_r, os_s, os_r, bm_s, bm, st_s, st_r, sc_s, sc_all, at_s, at_all, ds_s, ds_r, do_all,
    mx_s, mx, cg_s, cg, dq_s, dq_r, dkv_s, dkv_r,
    up_t, hv_t, hvg_t, gain_t, table, chunks, steps, dq_acc,
    send, recv, load,
):
    me = lax.axis_index("ctx")
    head = lax.axis_index("ch")
    y = lax.div(me, N)
    c = lax.rem(me, N)
    scale = 1.0 / math.sqrt(T)
    tap_scale = SEQ ** (-0.5)

    def y_peer(k):
        p = lax.rem(y + k, N)
        return p, (p * N + c, head)

    def c_peer(k):
        p = lax.rem(c + k, N)
        return p, (y * N + p, head)

    def h_peer(k):
        p = lax.rem(head + k, N)
        return p, (me, p)

    def all_peer(k):
        p = lax.rem(me + k, N * N)
        return p, (p, head)

    started = []

    def channel(dst):
        sem = len(started)
        started.append(dst)
        others = dst.shape[0] - 1

        def post(src, slot, device):
            pltpu.make_async_remote_copy(
                src_ref=src,
                dst_ref=dst.at[slot],
                send_sem=send.at[sem],
                recv_sem=recv.at[sem],
                device_id=device,
                device_id_type=MESH,
            ).start()

        def arrived():
            part = dst.at[pl.ds(0, others)]
            pltpu.make_async_copy(part, part, recv.at[sem]).wait()

        return post, arrived

    def spread(peer, src, dst, slot):
        post, arrived = channel(dst)

        def step(k, _):
            p, device = peer(k)
            post(src(p), slot, device)
            return 0

        lax.fori_loop(1, dst.shape[0], step, 0)
        return arrived

    barrier = pltpu.get_barrier_semaphore()

    def greet(peer):
        def step(k, _):
            pl.semaphore_signal(barrier, inc=1, device_id=peer(k)[1], device_id_type=MESH)
            return 0

        return step

    lax.fori_loop(1, N * N, greet(all_peer), 0)
    lax.fori_loop(1, N, greet(h_peer), 0)

    loads = [
        pltpu.make_async_copy(src, dst, load.at[i])
        for i, (src, dst) in enumerate(
            (
                (up_h, up_ref), (hq_h, hq_ref), (taps_h, taps_ref), (q_h, q_all.at[y]), (k_h, k_all.at[c]),
                (v_h, v_all.at[c]), (hv_h, hv_ref), (gain_h, gain_ref), (order_h, order_s), (order_h, order_v),
            )
        )
    ]
    for each in loads:
        each.start()
    for each in loads[0:3]:
        each.wait()
    up = up_ref[...].astype(F32)
    gated = (up * hq_ref[...].astype(F32)).astype(BF16)
    tg_s[...] = interleave(flip(gated).astype(BF16), flip(taps_ref[...]).astype(BF16)).reshape(N * N, 4, T)
    tg[me] = tg_s[me]
    for each in loads[3:]:
        each.wait()
    pl.semaphore_wait(barrier, N * N - 1 + N - 1)

    tg_here = spread(all_peer, lambda p: tg_s.at[p], tg, me)
    k_here = spread(c_peer, lambda p: k_all.at[c], k_all, c)
    q_here = spread(y_peer, lambda p: q_all.at[y], q_all, y)
    v_here = spread(c_peer, lambda p: v_all.at[c], v_all, c)

    up_t[...] = flip(up)
    hv_t[...] = flip(hv_ref[...])
    gain_t[...] = jnp.broadcast_to(gain_ref[...], (T, T)).T
    hvg_t[...] = hv_t[...] * gain_t[...]
    steps[:, 0:T, :] = jnp.zeros((2, T, T), F32)
    dq_acc[...] = jnp.zeros((T, N * T), F32)

    lane = iota((T, T), 1)
    line = iota((T, T), 0)
    order = jnp.broadcast_to(order_v[...].astype(F32), (8, T)).astype(BF16)
    place_f = [nn(order, one_hot(line == row_source(lane) * 2 + h))[0:1, :] for h in (0, 1)]
    place = [p.astype(jnp.int32) for p in place_f]
    place_t = [jnp.broadcast_to(p, (T, T)).T.astype(jnp.int32) for p in place_f]
    ours = [row_channel(lane) == j for j in (0, 1)]
    ours_t = [row_channel(line) == j for j in (0, 1)]
    here = lane & (HALF - 1)

    def lay_out(rows, turned, reverse):
        moved = [
            nn(rows, one_hot((line == h * HALF + (HALF - 1 - here if turned else here)) & ((lane >> 6) == e))).astype(BF16)
            for h in (0, 1)
            for e in (0, 1)
        ]
        for j in (0, 1):
            total = jnp.zeros((T, T), F32)
            for h in (0, 1):
                for e in (0, 1):
                    want = T - 1 - line + e if reverse else line - e
                    total = total + nn(one_hot(ours[j] & (place[h] == want)), moved[h * 2 + e])
            steps[j, T : 2 * T, :] = total

    def collect(results, spot, first, turned):
        total = jnp.zeros((T, T), F32)
        for h in (0, 1):
            mine = jnp.zeros((T, results[0].shape[1]), F32)
            for j in (0, 1):
                mine = mine + nn(one_hot(ours_t[j] & (spot[h] == lane)), results[j])
            wide = results[0].shape[1]
            a, b = iota((wide, T), 0), iota((wide, T), 1)
            inside = b & (HALF - 1)
            put = (a == first + (HALF - 1 - inside if turned else inside)) & ((b >> 6) == h)
            total = total + nn(mine.astype(BF16), one_hot(put))
        return total.astype(BF16)

    within = iota((1, 2 * T), 1)
    deep = iota((HALF, 2 * T), 0)

    def query_places(pair):
        base = within & (HALF - 1)
        spot = jnp.zeros((1, 2 * T), jnp.int32)
        for e in range(4):
            block = order_s[0, ((pair * 2 + e // 2) * N + c) * 2 + e % 2]
            spot = jnp.where((within >> 6) == e, block * HALF, spot)
        return spot + base

    def masked(tile, pair_q, spots):
        keys = k_all[pl.ds(2 * tile, 2)].reshape(2 * T, T)
        raw = nt(keys, pair_q) * (scale * LOG2E)
        out = []
        for e in range(4):
            block = order_s[0, y * 16 + tile * 4 + e]
            out.append(
                jnp.where(deep <= spots - block * HALF, raw[e * HALF : (e + 1) * HALF], HIDDEN)
            )
        return jnp.concatenate(out, axis=0)

    def attend(turn, _):
        pair = lax.rem(turn + lax.div(y, 2), 4)
        pair_q = q_all[pl.ds(pair * 2, 2)].reshape(2 * T, T)
        spots = query_places(pair)
        peak = jnp.full((1, 2 * T), HIDDEN, F32)
        for tile in range(4):
            part = masked(tile, pair_q, spots)
            scores[tile * 256 : (tile + 1) * 256, :] = part
            peak = jnp.maximum(peak, jnp.max(part, axis=0, keepdims=True))
        total = jnp.zeros((1, 2 * T), F32)
        out = jnp.zeros((T, 2 * T), F32)
        for tile in range(4):
            weights = jnp.exp2(scores[tile * 256 : (tile + 1) * 256, :] - peak)
            total = total + jnp.sum(weights, axis=0, keepdims=True)
            out = out + nn(vt[:, tile * 256 : (tile + 1) * 256], weights.astype(BF16))
        for e in (0, 1):
            p = pair * 2 + e
            lanes = slice(e * T, (e + 1) * T)
            o_s[p] = out[:, lanes].astype(BF16)
            os_s[p] = jnp.concatenate([peak[:, lanes], total[:, lanes]], axis=0)

            @pl.when(p != y)
            def _():
                os_post(os_s.at[p], y, (p * N + c, head))
                o_post(o_s.at[p], y, (p * N + c, head))

        return 0

    tg_here()
    both_rows = tg[...].reshape(2 * T, T)
    grads = separate(both_rows, 0)
    taps = separate(both_rows, 1)
    narrow_lane, narrow_line = iota((HALF, T), 1), iota((HALF, T), 0)
    narrow_ours = [row_channel(narrow_lane) == j for j in (0, 1)]
    for j in (0, 1):
        chunks[j] = nn(one_hot(narrow_ours[j] & (row_source(narrow_lane) == narrow_line)), taps)
    toeplitz(chunks, table, 0)
    lay_out(grads, False, True)
    backs = [(r * tap_scale).astype(BF16) for r in long_products(table, steps, HALF)]
    flipped_t = [T - 1 - p for p in place_t]
    bm_s[...] = collect(backs, flipped_t, 0, False).reshape(N * N, 2, T)
    bm[me] = bm_s[me]
    bm_here = spread(all_peer, lambda p: bm_s.at[p], bm, me)

    k_here()
    q_here()
    v_here()
    for i in range(N):
        vt[:, i * T : (i + 1) * T] = flip(v_all[i]).astype(BF16)
        kt[:, i * T : (i + 1) * T] = flip(k_all[i]).astype(BF16)
    os_post, os_here = channel(os_r)
    o_post, o_here = channel(o_r)
    lax.fori_loop(0, 4, attend, 0)
    o_r[y] = o_s[y]
    os_r[y] = os_s[y]

    flats = [jnp.zeros((HALF, T), F32)] * 2
    for h in (0, 1):
        for hh in (0, 1):
            turn = one_hot(((lane >> 6) == hh) & (line == h * HALF + HALF - 1 - here))
            turned = nn(grads, turn).astype(BF16)
            for j in (0, 1):
                pick = one_hot(narrow_ours[j] & (place[h] == T - 1 - 2 * narrow_line - hh))
                flats[j] = flats[j] + nn(pick, turned)
    for j in (0, 1):
        chunks[j] = flats[j]
    toeplitz(chunks, table, HALF)

    bm_here()
    back = bm[...].reshape(T, T).astype(F32)
    sc_s[...] = (back * hvg_t[...]).astype(BF16)
    sc_all[y] = sc_s[...]
    sc_here = spread(y_peer, lambda p: sc_s, sc_all, y)
    scaled = sc_s[...].astype(F32)

    os_here()
    o_here()
    peak = os_r[0, 0:1, :]
    for i in range(1, N):
        peak = jnp.maximum(peak, os_r[i, 0:1, :])
    total = jnp.zeros((1, T), F32)
    mix = jnp.zeros((T, T), F32)
    for i in range(N):
        factor = jnp.exp2(os_r[i, 0:1, :] - peak)
        total = total + factor * os_r[i, 1:2, :]
        mix = mix + factor * o_r[i].astype(F32)
    lse = peak + jnp.log2(total)
    at_s[...] = (mix / total).astype(BF16)
    act = at_s[...].astype(F32)
    st_s[...] = jnp.concatenate(
        [jnp.sum(act * act, axis=0, keepdims=True), jnp.sum(scaled * act, axis=0, keepdims=True)],
        axis=0,
    )
    st_r[head] = st_s[...]
    st_here = spread(h_peer, lambda p: st_s, st_r, head)
    at_all[y] = at_s[...]
    at_here = spread(y_peer, lambda p: at_s, at_all, y)

    st_here()
    sums = st_r[0]
    for i in range(1, N):
        sums = sums + st_r[i]
    inv_root = lax.rsqrt(sums[0:1, :] / WIDTH + 1e-06)
    pull = (inv_root * inv_root * inv_root) * (sums[1:2, :] / WIDTH)
    grad_att = (inv_root * scaled - act * pull).astype(BF16)
    delta = jnp.sum(grad_att.astype(F32) * act, axis=0, keepdims=True)
    ds_s[...] = jnp.concatenate([lse, delta, inv_root, pull], axis=0)
    ds_r[y] = ds_s[...]
    ds_here = spread(y_peer, lambda p: ds_s, ds_r, y)
    normed = act * inv_root * gain_t[...]
    mx_s[...] = (normed * hv_t[...]).astype(BF16).reshape(N * N, 2, T)
    mx[me] = mx_s[me]
    mx_here = spread(all_peer, lambda p: mx_s.at[p], mx, me)
    packed[4] = flip((back * normed).astype(BF16)).astype(BF16)

    sc_here()
    at_here()
    ds_here()
    for i in range(N):
        do_all[i] = (
            ds_r[i, 2:3, :] * sc_all[i].astype(F32) - at_all[i].astype(F32) * ds_r[i, 3:4, :]
        ).astype(BF16)
    dkv_post, dkv_here = channel(dkv_r)

    def grad(turn, _):
        tile = lax.rem(turn + lax.div(c, 2), 4)
        rows = pl.ds(pl.multiple_of(tile * 2 * T, 2 * T), 2 * T)
        tile_v = v_all[pl.ds(2 * tile, 2)].reshape(2 * T, T)
        dk = jnp.zeros((2 * T, T), F32)
        dv = jnp.zeros((2 * T, T), F32)
        for pair in range(4):
            pair_q = q_all[pair * 2 : pair * 2 + 2].reshape(2 * T, T)
            pair_do = jnp.concatenate([do_all[pair * 2], do_all[pair * 2 + 1]], axis=1)
            both = jnp.concatenate([ds_r[pair * 2], ds_r[pair * 2 + 1]], axis=1)
            probs = jnp.exp2(masked(tile, pair_q, query_places(pair)) - both[0:1, :])
            dprobs = nn(tile_v, pair_do)
            dscores = (probs * (dprobs - both[1:2, :])).astype(BF16)
            dv = dv + nt(probs.astype(BF16), pair_do)
            dk = dk + nn(dscores, pair_q)
            dq_acc[:, pair * 2 * T : (pair + 1) * 2 * T] += nn(kt[:, rows], dscores)
        dk = (dk * scale).astype(BF16)
        dv = dv.astype(BF16)
        for e in (0, 1):
            p = tile * 2 + e
            dkv_s[p, 0:T, :] = dk[e * T : (e + 1) * T]
            dkv_s[p, T : 2 * T, :] = dv[e * T : (e + 1) * T]

            @pl.when(p != c)
            def _():
                dkv_post(dkv_s.at[p], c, (y * N + p, head))

        return 0

    lax.fori_loop(0, 4, grad, 0)
    for i in range(N):
        dq_s[i] = (dq_acc[:, i * T : (i + 1) * T] * scale).astype(BF16)
    dq_here = spread(y_peer, lambda p: dq_s.at[p], dq_r, y)
    dq_r[y] = dq_s[y]
    dkv_r[c] = dkv_s[c]

    mx_here()
    lay_out(mx[...].reshape(T, T), True, False)
    lates = [(r * tap_scale).astype(BF16) for r in long_products(table, steps, T)]
    lag_t = [T - 1 - (row_source(line) * 2 + h) for h in (0, 1)]
    cg_s[...] = interleave(
        collect(lates, place_t, 0, True), collect(lates, lag_t, HALF, False)
    ).reshape(N * N, 4, T)
    cg[me] = cg_s[me]
    cg_here = spread(all_peer, lambda p: cg_s.at[p], cg, me)

    dq_here()
    grad_q = dq_r[0].astype(F32)
    for i in range(1, N):
        grad_q = grad_q + dq_r[i].astype(F32)
    packed[0] = grad_q.T.astype(BF16)
    dkv_here()
    grad_kv = dkv_r[0].astype(F32)
    for i in range(1, N):
        grad_kv = grad_kv + dkv_r[i].astype(F32)
    packed[1] = grad_kv[0:T].astype(BF16)
    packed[2] = grad_kv[T : 2 * T].astype(BF16)

    cg_here()
    results = cg[...].reshape(2 * T, T)
    packed[3] = flip(up_t[...] * separate(results, 0).astype(F32)).astype(BF16)
    packed[5] = flip(separate(results, 1)).astype(BF16)

    for sem, dst in enumerate(started):
        part = dst.at[pl.ds(0, dst.shape[0] - 1)]
        pltpu.make_async_copy(part, part, send.at[sem]).wait()


def unpack(packed, *rest):
    outs, done = rest[:-1], rest[-1]
    moves = [pltpu.make_async_copy(packed.at[i], out, done.at[i]) for i, out in enumerate(outs)]
    for move in moves:
        move.start()
    for move in moves:
        move.wait()


def per_device(queries, keys_in, values, hq, hv, taps, gain, upstream, order):
    def vmem(*shape, dtype=BF16):
        return pltpu.VMEM(shape, dtype)

    twos = vmem(N * N, 2, T)
    fours = vmem(N * N, 4, T)
    square = vmem(N, T, T)
    tall = vmem(N, 2 * T, T)
    lines = vmem(N, 2, T, dtype=F32)
    wide = vmem(T, T, dtype=F32)
    one = vmem(T, T)
    in_hbm = pl.BlockSpec(memory_space=pltpu.HBM)
    packed = pl.pallas_call(
        kernel,
        out_shape=jax.ShapeDtypeStruct((6, T, T), BF16),
        in_specs=[in_hbm] * 9,
        out_specs=pl.BlockSpec(memory_space=pltpu.VMEM),
        scratch_shapes=[
            pltpu.SMEM((1, T), jnp.int32), vmem(1, T, dtype=jnp.int32), one, one, one, vmem(1, T, dtype=F32), one,
            square, square, square, vmem(T, N * T), vmem(T, N * T), vmem(N * T, 2 * T, dtype=F32),
            fours, fours, square, square, lines, lines, twos, twos, vmem(2, T, dtype=F32), lines,
            one, square, one, square, vmem(4, T, dtype=F32), vmem(N, 4, T, dtype=F32), square,
            twos, twos, fours, fours, square, square, tall, tall,
            wide, wide, wide, wide, vmem(2, T, SEQ), vmem(2, HALF, T, dtype=F32), vmem(2, 2 * T, T, dtype=F32),
            vmem(T, N * T, dtype=F32),
            pltpu.SemaphoreType.DMA((15,)), pltpu.SemaphoreType.DMA((15,)), pltpu.SemaphoreType.DMA((10,)),
        ],
        compiler_params=pltpu.CompilerParams(
            collective_id=0, has_side_effects=True, vmem_limit_bytes=60 * 1024 * 1024
        ),
        name="pair_backward",
    )(order.reshape(1, -1), queries, keys_in, values, hq, hv, taps, gain.reshape(1, -1), upstream)
    return pl.pallas_call(
        unpack,
        out_shape=(jax.ShapeDtypeStruct((T, T), BF16),) * 6,
        in_specs=[in_hbm],
        out_specs=(in_hbm,) * 6,
        scratch_shapes=[pltpu.SemaphoreType.DMA((6,))],
        compiler_params=pltpu.CompilerParams(vmem_limit_bytes=60 * 1024 * 1024),
        name="unpack",
    )(packed)


def solution(mesh):
    rows = P("ctx", "ch")
    return jax.shard_map(
        per_device,
        mesh=mesh,
        in_specs=(rows,) * 6 + (P("ch"), rows, P()),
        out_specs=(rows,) * 6,
        check_vma=False,
    )
```

```python
import math

import jax
import jax.numpy as jnp
from jax import lax
from jax.experimental import pallas as pl
from jax.experimental.pallas import tpu as pltpu
from jax.sharding import PartitionSpec as P

T = 128
HALF = 64
N = 8
SEQ = T * N * N
WIDTH = 1024
LOG2E = 1.4426950408889634
HIDDEN = -1e30
MESH = pl.DeviceIdType.MESH
F32 = jnp.float32
BF16 = jnp.bfloat16


def nn(a, b):
    return lax.dot_general(a, b, (((1,), (0,)), ((), ())), preferred_element_type=F32)


def nt(a, b):
    return lax.dot_general(a, b, (((1,), (1,)), ((), ())), preferred_element_type=F32)


def iota(shape, dim):
    return lax.broadcasted_iota(jnp.int32, shape, dim)


def one_hot(cond):
    return jnp.where(cond, 1.0, 0.0).astype(BF16)


def flip(x):
    return x.astype(F32).T


def row_source(r):
    return r >> 1


def row_channel(r):
    return r & 1


def interleave(first, second):
    out, inn = iota((2 * T, T), 0), iota((2 * T, T), 1)
    return sum(
        nn(one_hot(out == (inn >> 1) * 4 + 2 * k + (inn & 1)), field) for k, field in enumerate((first, second))
    ).astype(BF16)


def separate(rows, k):
    out, inn = iota((T, 2 * T), 0), iota((T, 2 * T), 1)
    return nn(one_hot(inn == (out >> 1) * 4 + 2 * k + (out & 1)), rows).astype(BF16)


def toeplitz(chunks, table, first):
    ahead = iota((HALF, T), 1) >= iota((HALF, T), 0)

    def step(n, before):
        after = []
        for j in (0, 1):
            line = jnp.broadcast_to(chunks[j, pl.ds(n, 1), :], (HALF, T))
            now = pltpu.roll(line, 0, 1, stride=1, stride_axis=0)
            table[j, pl.ds(first, HALF), pl.ds(pl.multiple_of(n * T, T), T)] = jnp.where(
                ahead, now, before[j]
            ).astype(BF16)
            after.append(now)
        return tuple(after)

    empty = jnp.zeros((HALF, T), F32)
    lax.fori_loop(0, SEQ // T, step, (empty, empty), unroll=4)


def long_products(table, steps, wide):
    totals = [jnp.zeros((T, wide), F32)] * 2
    for part in range(4):
        top = part * 32
        rows = T - top

        def step(g, sums):
            p = part * 8 + g
            out = []
            for j in (0, 1):
                pair = [
                    steps[j, pl.ds(T + top - 4 * p - 2 * u, rows), :].astype(BF16) for u in (0, 1)
                ]
                right = table[j, 0:wide, pl.ds(pl.multiple_of(p * 256, 256), 256)]
                out.append(sums[j] + nt(jnp.concatenate(pair, axis=1), right))
            return tuple(out)

        sums = lax.fori_loop(0, 8, step, tuple(t[top:] for t in totals), unroll=2)
        if top:
            sums = [jnp.concatenate([totals[j][0:top], sums[j]], axis=0) for j in (0, 1)]
        totals = list(sums)
    return totals


def kernel(
    order_h, q_h, k_h, v_h, hq_h, hv_h, taps_h, gain_h, up_h,
    packed,
    order_s, order_v, hq_ref, hv_ref, taps_ref, gain_ref, up_ref,
    q_all, k_all, v_all, vt, kt, scores,
    tg_s, tg, o_s, o_r, os_s, os_r, bm_s, bm, st_s, st_r, sc_s, sc_all, at_s, at_all, ds_s, ds_r, do_all,
    mx_s, mx, cg_s, cg, dq_s, dq_r, dkv_s, dkv_r,
    up_t, hv_t, hvg_t, gain_t, table, chunks, steps, dq_acc,
    send, recv, load, grid_sem,
):
    me = lax.axis_index("ctx")
    head = lax.axis_index("ch")
    y = lax.div(me, N)
    c = lax.rem(me, N)
    scale = 1.0 / math.sqrt(T)
    tap_scale = SEQ ** (-0.5)

    def y_peer(k):
        p = lax.rem(y + k, N)
        return p, (p * N + c, head)

    def c_peer(k):
        p = lax.rem(c + k, N)
        return p, (y * N + p, head)

    def h_peer(k):
        p = lax.rem(head + k, N)
        return p, (me, p)

    def all_peer(k):
        p = lax.rem(me + k, N * N)
        return p, (p, head)

    started = []

    def channel(dst):
        sem = len(started)
        started.append(dst)
        others = dst.shape[0] - 1

        def post(src, slot, device):
            pltpu.make_async_remote_copy(
                src_ref=src,
                dst_ref=dst.at[slot],
                send_sem=send.at[sem],
                recv_sem=recv.at[sem],
                device_id=device,
                device_id_type=MESH,
            ).start()

        def arrived():
            part = dst.at[pl.ds(0, others)]
            pltpu.make_async_copy(part, part, recv.at[sem]).wait()

        return post, arrived

    def spread(peer, src, dst, slot):
        post, arrived = channel(dst)

        def step(k, _):
            p, device = peer(k)
            post(src(p), slot, device)
            return 0

        lax.fori_loop(1, dst.shape[0], step, 0)
        return arrived

    barrier = pltpu.get_barrier_semaphore()

    def greet(sem, peer):
        def step(k, _):
            pl.semaphore_signal(sem, inc=1, device_id=peer(k)[1], device_id_type=MESH)
            return 0

        return step

    for peer in (c_peer, y_peer, h_peer):
        lax.fori_loop(1, N, greet(barrier, peer), 0)

    loads = [
        pltpu.make_async_copy(src, dst, load.at[i])
        for i, (src, dst) in enumerate(
            (
                (up_h, up_ref), (hq_h, hq_ref), (taps_h, taps_ref), (q_h, q_all.at[y]), (k_h, k_all.at[c]),
                (v_h, v_all.at[c]), (hv_h, hv_ref), (gain_h, gain_ref), (order_h, order_s), (order_h, order_v),
            )
        )
    ]
    for each in loads:
        each.start()
    for each in loads[0:3]:
        each.wait()
    up = up_ref[...].astype(F32)
    gated = (up * hq_ref[...].astype(F32)).astype(BF16)
    tg_s[...] = interleave(flip(gated).astype(BF16), flip(taps_ref[...]).astype(BF16)).reshape(N * N, 4, T)
    tg[me] = tg_s[me]
    for each in loads[3:]:
        each.wait()
    pl.semaphore_wait(barrier, 3 * (N - 1))
    lax.fori_loop(1, N, greet(grid_sem, y_peer), 0)

    pl.semaphore_wait(grid_sem, N - 1)
    tg_here = spread(all_peer, lambda p: tg_s.at[p], tg, me)
    k_here = spread(c_peer, lambda p: k_all.at[c], k_all, c)
    q_here = spread(y_peer, lambda p: q_all.at[y], q_all, y)
    v_here = spread(c_peer, lambda p: v_all.at[c], v_all, c)

    up_t[...] = flip(up)
    hv_t[...] = flip(hv_ref[...])
    gain_t[...] = jnp.broadcast_to(gain_ref[...], (T, T)).T
    hvg_t[...] = hv_t[...] * gain_t[...]
    steps[:, 0:T, :] = jnp.zeros((2, T, T), F32)
    dq_acc[...] = jnp.zeros((T, N * T), F32)

    lane = iota((T, T), 1)
    line = iota((T, T), 0)
    order = jnp.broadcast_to(order_v[...].astype(F32), (8, T)).astype(BF16)
    place_f = [nn(order, one_hot(line == row_source(lane) * 2 + h))[0:1, :] for h in (0, 1)]
    place = [p.astype(jnp.int32) for p in place_f]
    place_t = [jnp.broadcast_to(p, (T, T)).T.astype(jnp.int32) for p in place_f]
    ours = [row_channel(lane) == j for j in (0, 1)]
    ours_t = [row_channel(line) == j for j in (0, 1)]
    here = lane & (HALF - 1)

    def lay_out(rows, turned, reverse):
        moved = [
            nn(rows, one_hot((line == h * HALF + (HALF - 1 - here if turned else here)) & ((lane >> 6) == e))).astype(BF16)
            for h in (0, 1)
            for e in (0, 1)
        ]
        for j in (0, 1):
            total = jnp.zeros((T, T), F32)
            for h in (0, 1):
                for e in (0, 1):
                    want = T - 1 - line + e if reverse else line - e
                    total = total + nn(one_hot(ours[j] & (place[h] == want)), moved[h * 2 + e])
            steps[j, T : 2 * T, :] = total

    def collect(results, spot, first, turned):
        total = jnp.zeros((T, T), F32)
        for h in (0, 1):
            mine = jnp.zeros((T, results[0].shape[1]), F32)
            for j in (0, 1):
                mine = mine + nn(one_hot(ours_t[j] & (spot[h] == lane)), results[j])
            wide = results[0].shape[1]
            a, b = iota((wide, T), 0), iota((wide, T), 1)
            inside = b & (HALF - 1)
            put = (a == first + (HALF - 1 - inside if turned else inside)) & ((b >> 6) == h)
            total = total + nn(mine.astype(BF16), one_hot(put))
        return total.astype(BF16)

    within = iota((1, 2 * T), 1)
    deep = iota((HALF, 2 * T), 0)

    def query_places(pair):
        base = within & (HALF - 1)
        spot = jnp.zeros((1, 2 * T), jnp.int32)
        for e in range(4):
            block = order_s[0, ((pair * 2 + e // 2) * N + c) * 2 + e % 2]
            spot = jnp.where((within >> 6) == e, block * HALF, spot)
        return spot + base

    def masked(tile, pair_q, spots):
        keys = k_all[pl.ds(2 * tile, 2)].reshape(2 * T, T)
        raw = nt(keys, pair_q) * (scale * LOG2E)
        out = []
        for e in range(4):
            block = order_s[0, y * 16 + tile * 4 + e]
            out.append(
                jnp.where(deep <= spots - block * HALF, raw[e * HALF : (e + 1) * HALF], HIDDEN)
            )
        return jnp.concatenate(out, axis=0)

    def attend(turn, _):
        pair = lax.rem(turn + lax.div(y, 2), 4)
        pair_q = q_all[pl.ds(pair * 2, 2)].reshape(2 * T, T)
        spots = query_places(pair)
        peak = jnp.full((1, 2 * T), HIDDEN, F32)
        for tile in range(4):
            part = masked(tile, pair_q, spots)
            scores[tile * 256 : (tile + 1) * 256, :] = part
            peak = jnp.maximum(peak, jnp.max(part, axis=0, keepdims=True))
        total = jnp.zeros((1, 2 * T), F32)
        out = jnp.zeros((T, 2 * T), F32)
        for tile in range(4):
            weights = jnp.exp2(scores[tile * 256 : (tile + 1) * 256, :] - peak)
            total = total + jnp.sum(weights, axis=0, keepdims=True)
            out = out + nn(vt[:, tile * 256 : (tile + 1) * 256], weights.astype(BF16))
        for e in (0, 1):
            p = pair * 2 + e
            lanes = slice(e * T, (e + 1) * T)
            o_s[p] = out[:, lanes].astype(BF16)
            os_s[p] = jnp.concatenate([peak[:, lanes], total[:, lanes]], axis=0)

            @pl.when(p != y)
            def _():
                os_post(os_s.at[p], y, (p * N + c, head))
                o_post(o_s.at[p], y, (p * N + c, head))

        return 0

    tg_here()
    both_rows = tg[...].reshape(2 * T, T)
    grads = separate(both_rows, 0)
    taps = separate(both_rows, 1)
    narrow_lane, narrow_line = iota((HALF, T), 1), iota((HALF, T), 0)
    narrow_ours = [row_channel(narrow_lane) == j for j in (0, 1)]
    for j in (0, 1):
        chunks[j] = nn(one_hot(narrow_ours[j] & (row_source(narrow_lane) == narrow_line)), taps)
    toeplitz(chunks, table, 0)
    lay_out(grads, False, True)
    backs = [(r * tap_scale).astype(BF16) for r in long_products(table, steps, HALF)]
    flipped_t = [T - 1 - p for p in place_t]
    bm_s[...] = collect(backs, flipped_t, 0, False).reshape(N * N, 2, T)
    bm[me] = bm_s[me]
    bm_here = spread(all_peer, lambda p: bm_s.at[p], bm, me)

    k_here()
    q_here()
    v_here()
    for i in range(N):
        vt[:, i * T : (i + 1) * T] = flip(v_all[i]).astype(BF16)
        kt[:, i * T : (i + 1) * T] = flip(k_all[i]).astype(BF16)
    os_post, os_here = channel(os_r)
    o_post, o_here = channel(o_r)
    lax.fori_loop(0, 4, attend, 0)
    o_r[y] = o_s[y]
    os_r[y] = os_s[y]

    flats = [jnp.zeros((HALF, T), F32)] * 2
    for h in (0, 1):
        for hh in (0, 1):
            turn = one_hot(((lane >> 6) == hh) & (line == h * HALF + HALF - 1 - here))
            turned = nn(grads, turn).astype(BF16)
            for j in (0, 1):
                pick = one_hot(narrow_ours[j] & (place[h] == T - 1 - 2 * narrow_line - hh))
                flats[j] = flats[j] + nn(pick, turned)
    for j in (0, 1):
        chunks[j] = flats[j]
    toeplitz(chunks, table, HALF)

    bm_here()
    back = bm[...].reshape(T, T).astype(F32)
    sc_s[...] = (back * hvg_t[...]).astype(BF16)
    sc_all[y] = sc_s[...]
    sc_here = spread(y_peer, lambda p: sc_s, sc_all, y)
    scaled = sc_s[...].astype(F32)

    os_here()
    o_here()
    peak = os_r[0, 0:1, :]
    for i in range(1, N):
        peak = jnp.maximum(peak, os_r[i, 0:1, :])
    total = jnp.zeros((1, T), F32)
    mix = jnp.zeros((T, T), F32)
    for i in range(N):
        factor = jnp.exp2(os_r[i, 0:1, :] - peak)
        total = total + factor * os_r[i, 1:2, :]
        mix = mix + factor * o_r[i].astype(F32)
    lse = peak + jnp.log2(total)
    at_s[...] = (mix / total).astype(BF16)
    act = at_s[...].astype(F32)
    st_s[...] = jnp.concatenate(
        [jnp.sum(act * act, axis=0, keepdims=True), jnp.sum(scaled * act, axis=0, keepdims=True)],
        axis=0,
    )
    st_r[head] = st_s[...]
    st_here = spread(h_peer, lambda p: st_s, st_r, head)
    at_all[y] = at_s[...]
    at_here = spread(y_peer, lambda p: at_s, at_all, y)

    st_here()
    sums = st_r[0]
    for i in range(1, N):
        sums = sums + st_r[i]
    inv_root = lax.rsqrt(sums[0:1, :] / WIDTH + 1e-06)
    pull = (inv_root * inv_root * inv_root) * (sums[1:2, :] / WIDTH)
    grad_att = (inv_root * scaled - act * pull).astype(BF16)
    delta = jnp.sum(grad_att.astype(F32) * act, axis=0, keepdims=True)
    ds_s[...] = jnp.concatenate([lse, delta, inv_root, pull], axis=0)
    ds_r[y] = ds_s[...]
    ds_here = spread(y_peer, lambda p: ds_s, ds_r, y)
    normed = act * inv_root * gain_t[...]
    mx_s[...] = (normed * hv_t[...]).astype(BF16).reshape(N * N, 2, T)
    mx[me] = mx_s[me]
    mx_here = spread(all_peer, lambda p: mx_s.at[p], mx, me)
    packed[4] = flip((back * normed).astype(BF16)).astype(BF16)

    sc_here()
    at_here()
    ds_here()
    for i in range(N):
        do_all[i] = (
            ds_r[i, 2:3, :] * sc_all[i].astype(F32) - at_all[i].astype(F32) * ds_r[i, 3:4, :]
        ).astype(BF16)
    dkv_post, dkv_here = channel(dkv_r)

    def grad(turn, _):
        tile = lax.rem(turn + lax.div(c, 2), 4)
        rows = pl.ds(pl.multiple_of(tile * 2 * T, 2 * T), 2 * T)
        tile_v = v_all[pl.ds(2 * tile, 2)].reshape(2 * T, T)
        dk = jnp.zeros((2 * T, T), F32)
        dv = jnp.zeros((2 * T, T), F32)
        for pair in range(4):
            pair_q = q_all[pair * 2 : pair * 2 + 2].reshape(2 * T, T)
            pair_do = jnp.concatenate([do_all[pair * 2], do_all[pair * 2 + 1]], axis=1)
            both = jnp.concatenate([ds_r[pair * 2], ds_r[pair * 2 + 1]], axis=1)
            probs = jnp.exp2(masked(tile, pair_q, query_places(pair)) - both[0:1, :])
            dprobs = nn(tile_v, pair_do)
            dscores = (probs * (dprobs - both[1:2, :])).astype(BF16)
            dv = dv + nt(probs.astype(BF16), pair_do)
            dk = dk + nn(dscores, pair_q)
            dq_acc[:, pair * 2 * T : (pair + 1) * 2 * T] += nn(kt[:, rows], dscores)
        dk = (dk * scale).astype(BF16)
        dv = dv.astype(BF16)
        for e in (0, 1):
            p = tile * 2 + e
            dkv_s[p, 0:T, :] = dk[e * T : (e + 1) * T]
            dkv_s[p, T : 2 * T, :] = dv[e * T : (e + 1) * T]

            @pl.when(p != c)
            def _():
                dkv_post(dkv_s.at[p], c, (y * N + p, head))

        return 0

    lax.fori_loop(0, 4, grad, 0)
    for i in range(N):
        dq_s[i] = (dq_acc[:, i * T : (i + 1) * T] * scale).astype(BF16)
    dq_here = spread(y_peer, lambda p: dq_s.at[p], dq_r, y)
    dq_r[y] = dq_s[y]
    dkv_r[c] = dkv_s[c]

    mx_here()
    lay_out(mx[...].reshape(T, T), True, False)
    lates = [(r * tap_scale).astype(BF16) for r in long_products(table, steps, T)]
    lag_t = [T - 1 - (row_source(line) * 2 + h) for h in (0, 1)]
    cg_s[...] = interleave(
        collect(lates, place_t, 0, True), collect(lates, lag_t, HALF, False)
    ).reshape(N * N, 4, T)
    cg[me] = cg_s[me]
    cg_here = spread(all_peer, lambda p: cg_s.at[p], cg, me)

    dq_here()
    grad_q = dq_r[0].astype(F32)
    for i in range(1, N):
        grad_q = grad_q + dq_r[i].astype(F32)
    packed[0] = grad_q.T.astype(BF16)
    dkv_here()
    grad_kv = dkv_r[0].astype(F32)
    for i in range(1, N):
        grad_kv = grad_kv + dkv_r[i].astype(F32)
    packed[1] = grad_kv[0:T].astype(BF16)
    packed[2] = grad_kv[T : 2 * T].astype(BF16)

    cg_here()
    results = cg[...].reshape(2 * T, T)
    packed[3] = flip(up_t[...] * separate(results, 0).astype(F32)).astype(BF16)
    packed[5] = flip(separate(results, 1)).astype(BF16)

    for sem, dst in enumerate(started):
        part = dst.at[pl.ds(0, dst.shape[0] - 1)]
        pltpu.make_async_copy(part, part, send.at[sem]).wait()


def unpack(packed, *outs):
    for i, out in enumerate(outs):
        out[...] = packed[i]


def per_device(queries, keys_in, values, hq, hv, taps, gain, upstream, order):
    def vmem(*shape, dtype=BF16):
        return pltpu.VMEM(shape, dtype)

    twos = vmem(N * N, 2, T)
    fours = vmem(N * N, 4, T)
    square = vmem(N, T, T)
    tall = vmem(N, 2 * T, T)
    lines = vmem(N, 2, T, dtype=F32)
    wide = vmem(T, T, dtype=F32)
    one = vmem(T, T)
    in_hbm = pl.BlockSpec(memory_space=pltpu.HBM)
    packed = pl.pallas_call(
        kernel,
        out_shape=jax.ShapeDtypeStruct((6, T, T), BF16),
        in_specs=[in_hbm] * 9,
        out_specs=pl.BlockSpec(memory_space=pltpu.VMEM),
        scratch_shapes=[
            pltpu.SMEM((1, T), jnp.int32), vmem(1, T, dtype=jnp.int32), one, one, one, vmem(1, T, dtype=F32), one,
            square, square, square, vmem(T, N * T), vmem(T, N * T), vmem(N * T, 2 * T, dtype=F32),
            fours, fours, square, square, lines, lines, twos, twos, vmem(2, T, dtype=F32), lines,
            one, square, one, square, vmem(4, T, dtype=F32), vmem(N, 4, T, dtype=F32), square,
            twos, twos, fours, fours, square, square, tall, tall,
            wide, wide, wide, wide, vmem(2, T, SEQ), vmem(2, HALF, T, dtype=F32), vmem(2, 2 * T, T, dtype=F32),
            vmem(T, N * T, dtype=F32),
            pltpu.SemaphoreType.DMA((15,)), pltpu.SemaphoreType.DMA((15,)), pltpu.SemaphoreType.DMA((10,)),
            pltpu.SemaphoreType.REGULAR,
        ],
        compiler_params=pltpu.CompilerParams(
            collective_id=0, has_side_effects=True, vmem_limit_bytes=60 * 1024 * 1024
        ),
        name="pair_backward",
    )(order.reshape(1, -1), queries, keys_in, values, hq, hv, taps, gain.reshape(1, -1), upstream)
    return pl.pallas_call(
        unpack,
        out_shape=(jax.ShapeDtypeStruct((T, T), BF16),) * 6,
        in_specs=[pl.BlockSpec(memory_space=pltpu.VMEM)],
        out_specs=(pl.BlockSpec(memory_space=pltpu.VMEM),) * 6,
        name="unpack",
    )(packed)


def solution(mesh):
    rows = P("ctx", "ch")
    return jax.shard_map(
        per_device,
        mesh=mesh,
        in_specs=(rows,) * 6 + (P("ch"), rows, P()),
        out_specs=(rows,) * 6,
        check_vma=False,
    )
```

```python
import math

import jax
import jax.numpy as jnp
from jax import lax
from jax.experimental import pallas as pl
from jax.experimental.pallas import tpu as pltpu
from jax.sharding import PartitionSpec as P

T = 128
HALF = 64
N = 8
SEQ = T * N * N
WIDTH = 1024
LOG2E = 1.4426950408889634
HIDDEN = -1e30
MESH = pl.DeviceIdType.MESH
F32 = jnp.float32
BF16 = jnp.bfloat16


def nn(a, b):
    return lax.dot_general(a, b, (((1,), (0,)), ((), ())), preferred_element_type=F32)


def nt(a, b):
    return lax.dot_general(a, b, (((1,), (1,)), ((), ())), preferred_element_type=F32)


def iota(shape, dim):
    return lax.broadcasted_iota(jnp.int32, shape, dim)


def one_hot(cond):
    return jnp.where(cond, 1.0, 0.0).astype(BF16)


def flip(x):
    return x.astype(F32).T


def row_source(r):
    return r >> 1


def row_channel(r):
    return r & 1


def interleave(first, second):
    out, inn = iota((2 * T, T), 0), iota((2 * T, T), 1)
    return sum(
        nn(one_hot(out == (inn >> 1) * 4 + 2 * k + (inn & 1)), field) for k, field in enumerate((first, second))
    ).astype(BF16)


def separate(rows, k):
    out, inn = iota((T, 2 * T), 0), iota((T, 2 * T), 1)
    return nn(one_hot(inn == (out >> 1) * 4 + 2 * k + (out & 1)), rows).astype(BF16)


def toeplitz(chunks, table, first):
    ahead = iota((HALF, T), 1) >= iota((HALF, T), 0)

    def step(n, before):
        after = []
        for j in (0, 1):
            line = jnp.broadcast_to(chunks[j, pl.ds(n, 1), :], (HALF, T))
            now = pltpu.roll(line, 0, 1, stride=1, stride_axis=0)
            table[j, pl.ds(first, HALF), pl.ds(pl.multiple_of(n * T, T), T)] = jnp.where(
                ahead, now, before[j]
            ).astype(BF16)
            after.append(now)
        return tuple(after)

    empty = jnp.zeros((HALF, T), F32)
    lax.fori_loop(0, SEQ // T, step, (empty, empty), unroll=4)


def long_products(table, steps, wide):
    totals = [None, None]
    for part in (3, 2, 1, 0):
        top = part * 32
        for j in (0, 1):
            pairs = [
                steps[j, T + top - d : 2 * T - d, :].astype(BF16) for d in range(top, top + 32, 2)
            ]
            right = table[j, 0:wide, part * 2048 : (part + 1) * 2048]
            now = nt(jnp.concatenate(pairs, axis=1), right)
            if totals[j] is not None:
                below = T - top - 32
                now = jnp.concatenate([now[0:32], now[32 : 32 + below] + totals[j]], axis=0)
            totals[j] = now
    return totals


def kernel(
    order_h, q_h, k_h, v_h, hq_h, hv_h, taps_h, gain_h, up_h,
    packed,
    order_s, order_v, hq_ref, hv_ref, taps_ref, gain_ref, up_ref,
    q_all, k_all, v_all, vt, kt,
    tg_s, tg, o_s, o_r, os_s, os_r, bm_s, bm, st_s, st_r, sc_s, sc_all, at_s, at_all, ds_s, ds_r, do_all,
    mx_s, mx, cg_s, cg, dq_s, dq_r, dkv_s, dkv_r,
    up_t, hv_t, hvg_t, gain_t, table, chunks, steps, dq_acc,
    send, recv, load, grid_sem,
):
    me = lax.axis_index("ctx")
    head = lax.axis_index("ch")
    y = lax.div(me, N)
    c = lax.rem(me, N)
    scale = 1.0 / math.sqrt(T)
    tap_scale = SEQ ** (-0.5)

    def y_peer(k):
        p = lax.rem(y + k, N)
        return p, (p * N + c, head)

    def c_peer(k):
        p = lax.rem(c + k, N)
        return p, (y * N + p, head)

    def h_peer(k):
        p = lax.rem(head + k, N)
        return p, (me, p)

    def all_peer(k):
        p = lax.rem(me + k, N * N)
        return p, (p, head)

    started = []

    def channel(dst):
        sem = len(started)
        started.append(dst)
        others = dst.shape[0] - 1

        def post(src, slot, device):
            pltpu.make_async_remote_copy(
                src_ref=src,
                dst_ref=dst.at[slot],
                send_sem=send.at[sem],
                recv_sem=recv.at[sem],
                device_id=device,
                device_id_type=MESH,
            ).start()

        def arrived():
            part = dst.at[pl.ds(0, others)]
            pltpu.make_async_copy(part, part, recv.at[sem]).wait()

        return post, arrived

    def spread(peer, src, dst, slot):
        post, arrived = channel(dst)

        def step(k, _):
            p, device = peer(k)
            post(src(p), slot, device)
            return 0

        lax.fori_loop(1, dst.shape[0], step, 0)
        return arrived

    barrier = pltpu.get_barrier_semaphore()

    def greet(sem, peer):
        def step(k, _):
            pl.semaphore_signal(sem, inc=1, device_id=peer(k)[1], device_id_type=MESH)
            return 0

        return step

    for peer in (c_peer, y_peer, h_peer):
        lax.fori_loop(1, N, greet(barrier, peer), 0)

    loads = [
        pltpu.make_async_copy(src, dst, load.at[i])
        for i, (src, dst) in enumerate(
            (
                (up_h, up_ref), (hq_h, hq_ref), (taps_h, taps_ref), (q_h, q_all.at[y]), (k_h, k_all.at[c]),
                (v_h, v_all.at[c]), (hv_h, hv_ref), (gain_h, gain_ref), (order_h, order_s), (order_h, order_v),
            )
        )
    ]
    for each in loads:
        each.start()
    for each in loads[0:3]:
        each.wait()
    up = up_ref[...].astype(F32)
    gated = (up * hq_ref[...].astype(F32)).astype(BF16)
    tg_s[...] = interleave(flip(gated).astype(BF16), flip(taps_ref[...]).astype(BF16)).reshape(N * N, 4, T)
    tg[me] = tg_s[me]
    for each in loads[3:]:
        each.wait()
    pl.semaphore_wait(barrier, 3 * (N - 1))
    lax.fori_loop(1, N, greet(grid_sem, y_peer), 0)

    pl.semaphore_wait(grid_sem, N - 1)
    tg_here = spread(all_peer, lambda p: tg_s.at[p], tg, me)
    k_here = spread(c_peer, lambda p: k_all.at[c], k_all, c)
    q_here = spread(y_peer, lambda p: q_all.at[y], q_all, y)
    v_here = spread(c_peer, lambda p: v_all.at[c], v_all, c)

    up_t[...] = flip(up)
    hv_t[...] = flip(hv_ref[...])
    gain_t[...] = jnp.broadcast_to(gain_ref[...], (T, T)).T
    hvg_t[...] = hv_t[...] * gain_t[...]
    steps[:, 0:T, :] = jnp.zeros((2, T, T), F32)

    lane = iota((T, T), 1)
    line = iota((T, T), 0)
    order = jnp.broadcast_to(order_v[...].astype(F32), (8, T)).astype(BF16)
    place_f = [nn(order, one_hot(line == row_source(lane) * 2 + h))[0:1, :] for h in (0, 1)]
    place = [p.astype(jnp.int32) for p in place_f]
    place_t = [jnp.broadcast_to(p, (T, T)).T.astype(jnp.int32) for p in place_f]
    ours = [row_channel(lane) == j for j in (0, 1)]
    ours_t = [row_channel(line) == j for j in (0, 1)]
    here = lane & (HALF - 1)

    def lay_out(rows, turned, reverse):
        moved = [
            nn(rows, one_hot((line == h * HALF + (HALF - 1 - here if turned else here)) & ((lane >> 6) == e))).astype(BF16)
            for h in (0, 1)
            for e in (0, 1)
        ]
        for j in (0, 1):
            total = jnp.zeros((T, T), F32)
            for h in (0, 1):
                for e in (0, 1):
                    want = T - 1 - line + e if reverse else line - e
                    total = total + nn(one_hot(ours[j] & (place[h] == want)), moved[h * 2 + e])
            steps[j, T : 2 * T, :] = total

    def collect(results, spot, first, turned):
        total = jnp.zeros((T, T), F32)
        for h in (0, 1):
            mine = jnp.zeros((T, results[0].shape[1]), F32)
            for j in (0, 1):
                mine = mine + nn(one_hot(ours_t[j] & (spot[h] == lane)), results[j])
            wide = results[0].shape[1]
            a, b = iota((wide, T), 0), iota((wide, T), 1)
            inside = b & (HALF - 1)
            put = (a == first + (HALF - 1 - inside if turned else inside)) & ((b >> 6) == h)
            total = total + nn(mine.astype(BF16), one_hot(put))
        return total.astype(BF16)

    within = iota((1, 2 * T), 1)
    deep = iota((HALF, 2 * T), 0)

    def query_places(pair):
        base = within & (HALF - 1)
        spot = jnp.zeros((1, 2 * T), jnp.int32)
        for e in range(4):
            block = order_s[0, (pair[e // 2] * N + c) * 2 + e % 2]
            spot = jnp.where((within >> 6) == e, block * HALF, spot)
        return spot + base

    def two(field, pair, axis=0):
        return jnp.concatenate([field[pair[0]], field[pair[1]]], axis=axis)

    def masked(keys, tile, pair_q, spots):
        raw = nt(keys, pair_q) * (scale * LOG2E)
        out = []
        for e in range(4):
            block = order_s[0, y * 16 + tile[e // 2] * 2 + e % 2]
            out.append(
                jnp.where(deep <= spots - block * HALF, raw[e * HALF : (e + 1) * HALF], HIDDEN)
            )
        return jnp.concatenate(out, axis=0)

    fixed = [(2 * t, 2 * t + 1) for t in range(4)]

    def others_first(own):
        return [tuple(lax.rem(own + 1 + 2 * t + e, N) for e in (0, 1)) for t in range(4)]

    def attend(turn, pair):
        pair_q = two(q_all, pair)
        spots = query_places(pair)
        parts = [masked(two(k_all, tile), tile, pair_q, spots) for tile in fixed]
        peak = jnp.max(jnp.maximum(jnp.maximum(parts[0], parts[1]), jnp.maximum(parts[2], parts[3])), axis=0, keepdims=True)
        total = jnp.zeros((1, 2 * T), F32)
        out = jnp.zeros((T, 2 * T), F32)
        for tile in range(4):
            weights = jnp.exp2(parts[tile] - peak)
            total = total + jnp.sum(weights, axis=0, keepdims=True)
            out = out + nn(vt[:, tile * 256 : (tile + 1) * 256], weights.astype(BF16))
        for e in (0, 1):
            p = pair[e]
            lanes = slice(e * T, (e + 1) * T)
            stats = jnp.concatenate([peak[:, lanes], total[:, lanes]], axis=0)
            if turn == 3 and e == 1:
                o_r[y] = out[:, lanes].astype(BF16)
                os_r[y] = stats
            else:
                o_s[p] = out[:, lanes].astype(BF16)
                os_s[p] = stats
                os_post(os_s.at[p], y, (p * N + c, head))
                o_post(o_s.at[p], y, (p * N + c, head))

    tg_here()
    both_rows = tg[...].reshape(2 * T, T)
    grads = separate(both_rows, 0)
    taps = separate(both_rows, 1)
    narrow_lane, narrow_line = iota((HALF, T), 1), iota((HALF, T), 0)
    narrow_ours = [row_channel(narrow_lane) == j for j in (0, 1)]
    for j in (0, 1):
        chunks[j] = nn(one_hot(narrow_ours[j] & (row_source(narrow_lane) == narrow_line)), taps)
    toeplitz(chunks, table, 0)
    lay_out(grads, False, True)
    backs = [(r * tap_scale).astype(BF16) for r in long_products(table, steps, HALF)]
    flipped_t = [T - 1 - p for p in place_t]
    bm_s[...] = collect(backs, flipped_t, 0, False).reshape(N * N, 2, T)
    bm[me] = bm_s[me]
    bm_here = spread(all_peer, lambda p: bm_s.at[p], bm, me)

    k_here()
    q_here()
    v_here()
    for i in range(N):
        vt[:, i * T : (i + 1) * T] = flip(v_all[i]).astype(BF16)
        kt[i] = flip(k_all[i]).astype(BF16)
    os_post, os_here = channel(os_r)
    o_post, o_here = channel(o_r)
    for turn, pair in enumerate(others_first(y)):
        attend(turn, pair)

    flats = [jnp.zeros((HALF, T), F32)] * 2
    for h in (0, 1):
        for hh in (0, 1):
            turn = one_hot(((lane >> 6) == hh) & (line == h * HALF + HALF - 1 - here))
            turned = nn(grads, turn).astype(BF16)
            for j in (0, 1):
                pick = one_hot(narrow_ours[j] & (place[h] == T - 1 - 2 * narrow_line - hh))
                flats[j] = flats[j] + nn(pick, turned)
    for j in (0, 1):
        chunks[j] = flats[j]
    toeplitz(chunks, table, HALF)

    bm_here()
    back = bm[...].reshape(T, T).astype(F32)
    sc_s[...] = (back * hvg_t[...]).astype(BF16)
    sc_all[y] = sc_s[...]
    sc_here = spread(y_peer, lambda p: sc_s, sc_all, y)
    scaled = sc_s[...].astype(F32)

    os_here()
    o_here()
    peak = os_r[0, 0:1, :]
    for i in range(1, N):
        peak = jnp.maximum(peak, os_r[i, 0:1, :])
    total = jnp.zeros((1, T), F32)
    mix = jnp.zeros((T, T), F32)
    for i in range(N):
        factor = jnp.exp2(os_r[i, 0:1, :] - peak)
        total = total + factor * os_r[i, 1:2, :]
        mix = mix + factor * o_r[i].astype(F32)
    lse = peak + jnp.log2(total)
    at_s[...] = (mix / total).astype(BF16)
    act = at_s[...].astype(F32)
    st_s[...] = jnp.concatenate(
        [jnp.sum(act * act, axis=0, keepdims=True), jnp.sum(scaled * act, axis=0, keepdims=True)],
        axis=0,
    )
    st_r[head] = st_s[...]
    st_here = spread(h_peer, lambda p: st_s, st_r, head)
    at_all[y] = at_s[...]
    at_here = spread(y_peer, lambda p: at_s, at_all, y)

    st_here()
    sums = st_r[0]
    for i in range(1, N):
        sums = sums + st_r[i]
    inv_root = lax.rsqrt(sums[0:1, :] / WIDTH + 1e-06)
    pull = (inv_root * inv_root * inv_root) * (sums[1:2, :] / WIDTH)
    grad_att = (inv_root * scaled - act * pull).astype(BF16)
    delta = jnp.sum(grad_att.astype(F32) * act, axis=0, keepdims=True)
    ds_s[...] = jnp.concatenate([lse, delta, inv_root, pull], axis=0)
    ds_r[y] = ds_s[...]
    ds_here = spread(y_peer, lambda p: ds_s, ds_r, y)
    normed = act * inv_root * gain_t[...]
    mx_s[...] = (normed * hv_t[...]).astype(BF16).reshape(N * N, 2, T)
    mx[me] = mx_s[me]
    mx_here = spread(all_peer, lambda p: mx_s.at[p], mx, me)
    packed[4] = flip((back * normed).astype(BF16)).astype(BF16)

    sc_here()
    at_here()
    ds_here()
    for i in range(N):
        do_all[i] = (
            ds_r[i, 2:3, :] * sc_all[i].astype(F32) - at_all[i].astype(F32) * ds_r[i, 3:4, :]
        ).astype(BF16)
    dkv_post, dkv_here = channel(dkv_r)

    def grad(turn, tile):
        tile_k, tile_v, tile_kt = two(k_all, tile), two(v_all, tile), two(kt, tile, 1)
        dk = jnp.zeros((2 * T, T), F32)
        dv = jnp.zeros((2 * T, T), F32)
        for pair in fixed:
            pair_q = two(q_all, pair)
            pair_do = two(do_all, pair, 1)
            both = two(ds_r, pair, 1)
            lanes = slice(pair[0] * T, (pair[1] + 1) * T)
            probs = jnp.exp2(masked(tile_k, tile, pair_q, query_places(pair)) - both[0:1, :])
            dprobs = nn(tile_v, pair_do)
            dscores = (probs * (dprobs - both[1:2, :])).astype(BF16)
            dv = dv + nt(probs.astype(BF16), pair_do)
            dk = dk + nn(dscores, pair_q)
            part = nn(tile_kt, dscores)
            dq_acc[:, lanes] = part if turn == 0 else dq_acc[:, lanes] + part
        dkv = (dk * scale).astype(BF16), dv.astype(BF16)
        for e in (0, 1):
            p = tile[e]
            own = turn == 3 and e == 1
            for i, field in enumerate(dkv):
                (dkv_r if own else dkv_s)[p, i * T : (i + 1) * T, :] = field[e * T : (e + 1) * T]
            if not own:
                dkv_post(dkv_s.at[p], c, (y * N + p, head))

    for turn, tile in enumerate(others_first(c)):
        grad(turn, tile)
    for i in range(N):
        dq_s[i] = (dq_acc[:, i * T : (i + 1) * T] * scale).astype(BF16)
    dq_here = spread(y_peer, lambda p: dq_s.at[p], dq_r, y)
    dq_r[y] = dq_s[y]

    mx_here()
    lay_out(mx[...].reshape(T, T), True, False)
    lates = [(r * tap_scale).astype(BF16) for r in long_products(table, steps, T)]
    lag_t = [T - 1 - (row_source(line) * 2 + h) for h in (0, 1)]
    cg_s[...] = interleave(
        collect(lates, place_t, 0, True), collect(lates, lag_t, HALF, False)
    ).reshape(N * N, 4, T)
    cg[me] = cg_s[me]
    cg_here = spread(all_peer, lambda p: cg_s.at[p], cg, me)

    dq_here()
    grad_q = dq_r[0].astype(F32)
    for i in range(1, N):
        grad_q = grad_q + dq_r[i].astype(F32)
    packed[0] = grad_q.T.astype(BF16)
    dkv_here()
    grad_kv = dkv_r[0].astype(F32)
    for i in range(1, N):
        grad_kv = grad_kv + dkv_r[i].astype(F32)
    packed[1] = grad_kv[0:T].astype(BF16)
    packed[2] = grad_kv[T : 2 * T].astype(BF16)

    cg_here()
    results = cg[...].reshape(2 * T, T)
    packed[3] = flip(up_t[...] * separate(results, 0).astype(F32)).astype(BF16)
    packed[5] = flip(separate(results, 1)).astype(BF16)

    for sem, dst in enumerate(started):
        part = dst.at[pl.ds(0, dst.shape[0] - 1)]
        pltpu.make_async_copy(part, part, send.at[sem]).wait()


def unpack(packed, *outs):
    for i, out in enumerate(outs):
        out[...] = packed[i]


def per_device(queries, keys_in, values, hq, hv, taps, gain, upstream, order):
    def vmem(*shape, dtype=BF16):
        return pltpu.VMEM(shape, dtype)

    twos = vmem(N * N, 2, T)
    fours = vmem(N * N, 4, T)
    square = vmem(N, T, T)
    tall = vmem(N, 2 * T, T)
    lines = vmem(N, 2, T, dtype=F32)
    wide = vmem(T, T, dtype=F32)
    one = vmem(T, T)
    in_hbm = pl.BlockSpec(memory_space=pltpu.HBM)
    packed = pl.pallas_call(
        kernel,
        out_shape=jax.ShapeDtypeStruct((6, T, T), BF16),
        in_specs=[in_hbm] * 9,
        out_specs=pl.BlockSpec(memory_space=pltpu.VMEM),
        scratch_shapes=[
            pltpu.SMEM((1, T), jnp.int32), vmem(1, T, dtype=jnp.int32), one, one, one, vmem(1, T, dtype=F32), one,
            square, square, square, vmem(T, N * T), square,
            fours, fours, square, square, lines, lines, twos, twos, vmem(2, T, dtype=F32), lines,
            one, square, one, square, vmem(4, T, dtype=F32), vmem(N, 4, T, dtype=F32), square,
            twos, twos, fours, fours, square, square, tall, tall,
            wide, wide, wide, wide, vmem(2, T, SEQ), vmem(2, HALF, T, dtype=F32), vmem(2, 2 * T, T, dtype=F32),
            vmem(T, N * T, dtype=F32),
            pltpu.SemaphoreType.DMA((15,)), pltpu.SemaphoreType.DMA((15,)), pltpu.SemaphoreType.DMA((10,)),
            pltpu.SemaphoreType.REGULAR,
        ],
        compiler_params=pltpu.CompilerParams(
            collective_id=0, has_side_effects=True, vmem_limit_bytes=60 * 1024 * 1024
        ),
        name="pair_backward",
    )(order.reshape(1, -1), queries, keys_in, values, hq, hv, taps, gain.reshape(1, -1), upstream)
    return pl.pallas_call(
        unpack,
        out_shape=(jax.ShapeDtypeStruct((T, T), BF16),) * 6,
        in_specs=[pl.BlockSpec(memory_space=pltpu.VMEM)],
        out_specs=(pl.BlockSpec(memory_space=pltpu.VMEM),) * 6,
        name="unpack",
    )(packed)


def solution(mesh):
    rows = P("ctx", "ch")
    return jax.shard_map(
        per_device,
        mesh=mesh,
        in_specs=(rows,) * 6 + (P("ch"), rows, P()),
        out_specs=(rows,) * 6,
        check_vma=False,
    )
```

```python
import math

import jax
import jax.numpy as jnp
from jax import lax
from jax.experimental import pallas as pl
from jax.experimental.pallas import tpu as pltpu
from jax.sharding import PartitionSpec as P

T = 128
HALF = 64
N = 8
SEQ = T * N * N
WIDTH = 1024
LOG2E = 1.4426950408889634
HIDDEN = -1e30
MESH = pl.DeviceIdType.MESH
F32 = jnp.float32
BF16 = jnp.bfloat16


def nn(a, b):
    return lax.dot_general(a, b, (((1,), (0,)), ((), ())), preferred_element_type=F32)


def nt(a, b):
    return lax.dot_general(a, b, (((1,), (1,)), ((), ())), preferred_element_type=F32)


def iota(shape, dim):
    return lax.broadcasted_iota(jnp.int32, shape, dim)


def one_hot(cond):
    return jnp.where(cond, 1.0, 0.0).astype(BF16)


def flip(x):
    return x.astype(F32).T


def row_source(r):
    return r >> 1


def row_channel(r):
    return r & 1


def interleave(first, second):
    out, inn = iota((2 * T, T), 0), iota((2 * T, T), 1)
    return sum(
        nn(one_hot(out == (inn >> 1) * 4 + 2 * k + (inn & 1)), field) for k, field in enumerate((first, second))
    ).astype(BF16)


def separate(rows, k):
    out, inn = iota((T, 2 * T), 0), iota((T, 2 * T), 1)
    return nn(one_hot(inn == (out >> 1) * 4 + 2 * k + (out & 1)), rows).astype(BF16)


def toeplitz(chunks, table, first):
    ahead = iota((HALF, T), 1) >= iota((HALF, T), 0)

    def step(n, before):
        after = []
        for j in (0, 1):
            line = jnp.broadcast_to(chunks[j, pl.ds(n, 1), :], (HALF, T))
            now = pltpu.roll(line, 0, 1, stride=1, stride_axis=0)
            table[j, pl.ds(first, HALF), pl.ds(pl.multiple_of(n * T, T), T)] = jnp.where(
                ahead, now, before[j]
            ).astype(BF16)
            after.append(now)
        return tuple(after)

    empty = jnp.zeros((HALF, T), F32)
    lax.fori_loop(0, SEQ // T, step, (empty, empty), unroll=16)


def long_products(table, steps, wide):
    totals = [None, None]
    for part in (3, 2, 1, 0):
        top = part * 32
        for j in (0, 1):
            pairs = [
                steps[j, T + top - d : 2 * T - d, :].astype(BF16) for d in range(top, top + 32, 2)
            ]
            right = table[j, 0:wide, part * 2048 : (part + 1) * 2048]
            now = nt(jnp.concatenate(pairs, axis=1), right)
            if totals[j] is not None:
                below = T - top - 32
                now = jnp.concatenate([now[0:32], now[32 : 32 + below] + totals[j]], axis=0)
            totals[j] = now
    return totals


def kernel(
    order_h, q_h, k_h, v_h, hq_h, hv_h, taps_h, gain_h, up_h,
    packed,
    order_s, order_v, hq_ref, hv_ref, taps_ref, gain_ref, up_ref,
    q_all, k_all, v_all, vt, kt,
    tg_s, tg, o_s, o_r, os_s, os_r, bm_s, bm, st_s, st_r, sc_s, sc_all, at_s, at_all, ds_s, ds_r, do_all,
    mx_s, mx, cg_s, cg, dq_s, dq_r, dkv_s, dkv_r,
    up_t, hv_t, hvg_t, gain_t, table, chunks, steps, dq_acc,
    outs, send, recv, load, grid_sem, store,
):
    me = lax.axis_index("ctx")
    head = lax.axis_index("ch")
    y = lax.div(me, N)
    c = lax.rem(me, N)
    scale = 1.0 / math.sqrt(T)
    tap_scale = SEQ ** (-0.5)

    def y_peer(k):
        p = lax.rem(y + k, N)
        return p, (p * N + c, head)

    def c_peer(k):
        p = lax.rem(c + k, N)
        return p, (y * N + p, head)

    def h_peer(k):
        p = lax.rem(head + k, N)
        return p, (me, p)

    def all_peer(k):
        p = lax.rem(me + k, N * N)
        return p, (p, head)

    started = []

    def channel(dst):
        sem = len(started)
        started.append(dst)
        others = dst.shape[0] - 1

        def post(src, slot, device):
            pltpu.make_async_remote_copy(
                src_ref=src,
                dst_ref=dst.at[slot],
                send_sem=send.at[sem],
                recv_sem=recv.at[sem],
                device_id=device,
                device_id_type=MESH,
            ).start()

        def arrived():
            part = dst.at[pl.ds(0, others)]
            pltpu.make_async_copy(part, part, recv.at[sem]).wait()

        return post, arrived

    def spread(peer, src, dst, slot):
        post, arrived = channel(dst)

        def step(k, _):
            p, device = peer(k)
            post(src(p), slot, device)
            return 0

        lax.fori_loop(1, dst.shape[0], step, 0)
        return arrived

    barrier = pltpu.get_barrier_semaphore()

    def greet(sem, peer):
        def step(k, _):
            pl.semaphore_signal(sem, inc=1, device_id=peer(k)[1], device_id_type=MESH)
            return 0

        return step

    for peer in (c_peer, y_peer, h_peer):
        lax.fori_loop(1, N, greet(barrier, peer), 0)

    moves = [pltpu.make_async_copy(outs.at[i], packed.at[i], store.at[i]) for i in range(6)]
    loads = [
        pltpu.make_async_copy(src, dst, load.at[i])
        for i, (src, dst) in enumerate(
            (
                (up_h, up_ref), (hq_h, hq_ref), (taps_h, taps_ref), (q_h, q_all.at[y]), (k_h, k_all.at[c]),
                (v_h, v_all.at[c]), (hv_h, hv_ref), (gain_h, gain_ref), (order_h, order_s), (order_h, order_v),
            )
        )
    ]
    for each in loads:
        each.start()
    for each in loads[0:3]:
        each.wait()
    up = up_ref[...].astype(F32)
    gated = (up * hq_ref[...].astype(F32)).astype(BF16)
    tg_s[...] = interleave(flip(gated).astype(BF16), flip(taps_ref[...]).astype(BF16)).reshape(N * N, 4, T)
    tg[me] = tg_s[me]
    for each in loads[3:]:
        each.wait()
    pl.semaphore_wait(barrier, 3 * (N - 1))
    lax.fori_loop(1, N, greet(grid_sem, y_peer), 0)

    pl.semaphore_wait(grid_sem, N - 1)
    tg_here = spread(all_peer, lambda p: tg_s.at[p], tg, me)
    k_here = spread(c_peer, lambda p: k_all.at[c], k_all, c)
    q_here = spread(y_peer, lambda p: q_all.at[y], q_all, y)
    v_here = spread(c_peer, lambda p: v_all.at[c], v_all, c)

    up_t[...] = flip(up)
    hv_t[...] = flip(hv_ref[...])
    gain_t[...] = jnp.broadcast_to(gain_ref[...], (T, T)).T
    hvg_t[...] = hv_t[...] * gain_t[...]
    steps[:, 0:T, :] = jnp.zeros((2, T, T), F32)

    lane = iota((T, T), 1)
    line = iota((T, T), 0)
    order = jnp.broadcast_to(order_v[...].astype(F32), (8, T)).astype(BF16)
    place_f = [nn(order, one_hot(line == row_source(lane) * 2 + h))[0:1, :] for h in (0, 1)]
    place = [p.astype(jnp.int32) for p in place_f]
    place_t = [jnp.broadcast_to(p, (T, T)).T.astype(jnp.int32) for p in place_f]
    ours = [row_channel(lane) == j for j in (0, 1)]
    ours_t = [row_channel(line) == j for j in (0, 1)]
    here = lane & (HALF - 1)

    def lay_out(rows, turned, reverse):
        moved = [
            nn(rows, one_hot((line == h * HALF + (HALF - 1 - here if turned else here)) & ((lane >> 6) == e))).astype(BF16)
            for h in (0, 1)
            for e in (0, 1)
        ]
        for j in (0, 1):
            total = jnp.zeros((T, T), F32)
            for h in (0, 1):
                for e in (0, 1):
                    want = T - 1 - line + e if reverse else line - e
                    total = total + nn(one_hot(ours[j] & (place[h] == want)), moved[h * 2 + e])
            steps[j, T : 2 * T, :] = total

    def collect(results, spot, first, turned):
        total = jnp.zeros((T, T), F32)
        for h in (0, 1):
            mine = jnp.zeros((T, results[0].shape[1]), F32)
            for j in (0, 1):
                mine = mine + nn(one_hot(ours_t[j] & (spot[h] == lane)), results[j])
            wide = results[0].shape[1]
            a, b = iota((wide, T), 0), iota((wide, T), 1)
            inside = b & (HALF - 1)
            put = (a == first + (HALF - 1 - inside if turned else inside)) & ((b >> 6) == h)
            total = total + nn(mine.astype(BF16), one_hot(put))
        return total.astype(BF16)

    within = iota((1, 2 * T), 1)
    deep = iota((HALF, 2 * T), 0)

    def query_places(pair):
        base = within & (HALF - 1)
        spot = jnp.zeros((1, 2 * T), jnp.int32)
        for e in range(4):
            block = order_s[0, (pair[e // 2] * N + c) * 2 + e % 2]
            spot = jnp.where((within >> 6) == e, block * HALF, spot)
        return spot + base

    def two(field, pair, axis=0):
        return jnp.concatenate([field[pair[0]], field[pair[1]]], axis=axis)

    def masked(keys, tile, pair_q, spots):
        raw = nt(keys, pair_q) * (scale * LOG2E)
        out = []
        for e in range(4):
            block = order_s[0, y * 16 + tile[e // 2] * 2 + e % 2]
            out.append(
                jnp.where(deep <= spots - block * HALF, raw[e * HALF : (e + 1) * HALF], HIDDEN)
            )
        return jnp.concatenate(out, axis=0)

    fixed = [(2 * t, 2 * t + 1) for t in range(4)]

    def others_first(own):
        return [tuple(lax.rem(own + 1 + 2 * t + e, N) for e in (0, 1)) for t in range(4)]

    def attend(turn, pair):
        pair_q = two(q_all, pair)
        spots = query_places(pair)
        parts = [masked(two(k_all, tile), tile, pair_q, spots) for tile in fixed]
        peak = jnp.max(jnp.maximum(jnp.maximum(parts[0], parts[1]), jnp.maximum(parts[2], parts[3])), axis=0, keepdims=True)
        total = jnp.zeros((1, 2 * T), F32)
        out = jnp.zeros((T, 2 * T), F32)
        for tile in range(4):
            weights = jnp.exp2(parts[tile] - peak)
            total = total + jnp.sum(weights, axis=0, keepdims=True)
            out = out + nn(vt[:, tile * 256 : (tile + 1) * 256], weights.astype(BF16))
        for e in (0, 1):
            p = pair[e]
            lanes = slice(e * T, (e + 1) * T)
            stats = jnp.concatenate([peak[:, lanes], total[:, lanes]], axis=0)
            if turn == 3 and e == 1:
                o_r[y] = out[:, lanes].astype(BF16)
                os_r[y] = stats
            else:
                o_s[p] = out[:, lanes].astype(BF16)
                os_s[p] = stats
                os_post(os_s.at[p], y, (p * N + c, head))
                o_post(o_s.at[p], y, (p * N + c, head))

    tg_here()
    both_rows = tg[...].reshape(2 * T, T)
    grads = separate(both_rows, 0)
    taps = separate(both_rows, 1)
    narrow_lane, narrow_line = iota((HALF, T), 1), iota((HALF, T), 0)
    narrow_ours = [row_channel(narrow_lane) == j for j in (0, 1)]
    for j in (0, 1):
        chunks[j] = nn(one_hot(narrow_ours[j] & (row_source(narrow_lane) == narrow_line)), taps)
    toeplitz(chunks, table, 0)
    lay_out(grads, False, True)
    backs = [(r * tap_scale).astype(BF16) for r in long_products(table, steps, HALF)]
    flipped_t = [T - 1 - p for p in place_t]
    bm_s[...] = collect(backs, flipped_t, 0, False).reshape(N * N, 2, T)
    bm[me] = bm_s[me]
    bm_here = spread(all_peer, lambda p: bm_s.at[p], bm, me)

    k_here()
    q_here()
    v_here()
    for i in range(N):
        vt[:, i * T : (i + 1) * T] = flip(v_all[i]).astype(BF16)
        kt[i] = flip(k_all[i]).astype(BF16)
    os_post, os_here = channel(os_r)
    o_post, o_here = channel(o_r)
    for turn, pair in enumerate(others_first(y)):
        attend(turn, pair)

    bm_here()
    back = bm[...].reshape(T, T).astype(F32)
    sc_s[...] = (back * hvg_t[...]).astype(BF16)
    sc_all[y] = sc_s[...]
    sc_here = spread(y_peer, lambda p: sc_s, sc_all, y)
    scaled = sc_s[...].astype(F32)

    flats = [jnp.zeros((HALF, T), F32)] * 2
    for h in (0, 1):
        for hh in (0, 1):
            turn = one_hot(((lane >> 6) == hh) & (line == h * HALF + HALF - 1 - here))
            turned = nn(grads, turn).astype(BF16)
            for j in (0, 1):
                pick = one_hot(narrow_ours[j] & (place[h] == T - 1 - 2 * narrow_line - hh))
                flats[j] = flats[j] + nn(pick, turned)
    for j in (0, 1):
        chunks[j] = flats[j]
    toeplitz(chunks, table, HALF)

    os_here()
    o_here()
    peak = os_r[0, 0:1, :]
    for i in range(1, N):
        peak = jnp.maximum(peak, os_r[i, 0:1, :])
    total = jnp.zeros((1, T), F32)
    mix = jnp.zeros((T, T), F32)
    for i in range(N):
        factor = jnp.exp2(os_r[i, 0:1, :] - peak)
        total = total + factor * os_r[i, 1:2, :]
        mix = mix + factor * o_r[i].astype(F32)
    lse = peak + jnp.log2(total)
    at_s[...] = (mix / total).astype(BF16)
    act = at_s[...].astype(F32)
    st_s[...] = jnp.concatenate(
        [jnp.sum(act * act, axis=0, keepdims=True), jnp.sum(scaled * act, axis=0, keepdims=True)],
        axis=0,
    )
    st_r[head] = st_s[...]
    st_here = spread(h_peer, lambda p: st_s, st_r, head)
    at_all[y] = at_s[...]
    at_here = spread(y_peer, lambda p: at_s, at_all, y)

    st_here()
    sums = st_r[0]
    for i in range(1, N):
        sums = sums + st_r[i]
    inv_root = lax.rsqrt(sums[0:1, :] / WIDTH + 1e-06)
    pull = (inv_root * inv_root * inv_root) * (sums[1:2, :] / WIDTH)
    grad_att = (inv_root * scaled - act * pull).astype(BF16)
    delta = jnp.sum(grad_att.astype(F32) * act, axis=0, keepdims=True)
    ds_s[...] = jnp.concatenate([lse, delta, inv_root, pull], axis=0)
    ds_r[y] = ds_s[...]
    ds_here = spread(y_peer, lambda p: ds_s, ds_r, y)
    normed = act * inv_root * gain_t[...]
    mx_s[...] = (normed * hv_t[...]).astype(BF16).reshape(N * N, 2, T)
    mx[me] = mx_s[me]
    mx_here = spread(all_peer, lambda p: mx_s.at[p], mx, me)
    outs[4] = flip((back * normed).astype(BF16)).astype(BF16)
    moves[4].start()

    sc_here()
    at_here()
    ds_here()
    for i in range(N):
        do_all[i] = (
            ds_r[i, 2:3, :] * sc_all[i].astype(F32) - at_all[i].astype(F32) * ds_r[i, 3:4, :]
        ).astype(BF16)
    dkv_post, dkv_here = channel(dkv_r)

    def grad(turn, tile):
        tile_k, tile_v, tile_kt = two(k_all, tile), two(v_all, tile), two(kt, tile, 1)
        dk = jnp.zeros((2 * T, T), F32)
        dv = jnp.zeros((2 * T, T), F32)
        for pair in fixed:
            pair_q = two(q_all, pair)
            pair_do = two(do_all, pair, 1)
            both = two(ds_r, pair, 1)
            lanes = slice(pair[0] * T, (pair[1] + 1) * T)
            probs = jnp.exp2(masked(tile_k, tile, pair_q, query_places(pair)) - both[0:1, :])
            dprobs = nn(tile_v, pair_do)
            dscores = (probs * (dprobs - both[1:2, :])).astype(BF16)
            dv = dv + nt(probs.astype(BF16), pair_do)
            dk = dk + nn(dscores, pair_q)
            part = nn(tile_kt, dscores)
            dq_acc[:, lanes] = part if turn == 0 else dq_acc[:, lanes] + part
        dkv = (dk * scale).astype(BF16), dv.astype(BF16)
        for e in (0, 1):
            p = tile[e]
            own = turn == 3 and e == 1
            for i, field in enumerate(dkv):
                (dkv_r if own else dkv_s)[p, i * T : (i + 1) * T, :] = field[e * T : (e + 1) * T]
            if not own:
                dkv_post(dkv_s.at[p], c, (y * N + p, head))

    for turn, tile in enumerate(others_first(c)):
        grad(turn, tile)
    for i in range(N):
        dq_s[i] = (dq_acc[:, i * T : (i + 1) * T] * scale).astype(BF16)
    dq_here = spread(y_peer, lambda p: dq_s.at[p], dq_r, y)
    dq_r[y] = dq_s[y]

    mx_here()
    lay_out(mx[...].reshape(T, T), True, False)
    lates = [(r * tap_scale).astype(BF16) for r in long_products(table, steps, T)]
    lag_t = [T - 1 - (row_source(line) * 2 + h) for h in (0, 1)]
    cg_s[...] = interleave(
        collect(lates, place_t, 0, True), collect(lates, lag_t, HALF, False)
    ).reshape(N * N, 4, T)
    cg[me] = cg_s[me]
    cg_here = spread(all_peer, lambda p: cg_s.at[p], cg, me)

    dq_here()
    grad_q = dq_r[0].astype(F32)
    for i in range(1, N):
        grad_q = grad_q + dq_r[i].astype(F32)
    outs[0] = grad_q.T.astype(BF16)
    moves[0].start()
    dkv_here()
    grad_kv = dkv_r[0].astype(F32)
    for i in range(1, N):
        grad_kv = grad_kv + dkv_r[i].astype(F32)
    outs[1] = grad_kv[0:T].astype(BF16)
    moves[1].start()
    outs[2] = grad_kv[T : 2 * T].astype(BF16)
    moves[2].start()

    cg_here()
    results = cg[...].reshape(2 * T, T)
    outs[3] = flip(up_t[...] * separate(results, 0).astype(F32)).astype(BF16)
    moves[3].start()
    outs[5] = flip(separate(results, 1)).astype(BF16)
    moves[5].start()

    for sem, dst in enumerate(started):
        part = dst.at[pl.ds(0, dst.shape[0] - 1)]
        pltpu.make_async_copy(part, part, send.at[sem]).wait()
    for move in moves:
        move.wait()


def unpack(packed, *outs):
    for i, out in enumerate(outs):
        out[...] = packed[i]


def per_device(queries, keys_in, values, hq, hv, taps, gain, upstream, order):
    def vmem(*shape, dtype=BF16):
        return pltpu.VMEM(shape, dtype)

    twos = vmem(N * N, 2, T)
    fours = vmem(N * N, 4, T)
    square = vmem(N, T, T)
    tall = vmem(N, 2 * T, T)
    lines = vmem(N, 2, T, dtype=F32)
    wide = vmem(T, T, dtype=F32)
    one = vmem(T, T)
    in_hbm = pl.BlockSpec(memory_space=pltpu.HBM)
    packed = pl.pallas_call(
        kernel,
        out_shape=jax.ShapeDtypeStruct((6, T, T), BF16),
        in_specs=[in_hbm] * 9,
        out_specs=in_hbm,
        scratch_shapes=[
            pltpu.SMEM((1, T), jnp.int32), vmem(1, T, dtype=jnp.int32), one, one, one, vmem(1, T, dtype=F32), one,
            square, square, square, vmem(T, N * T), square,
            fours, fours, square, square, lines, lines, twos, twos, vmem(2, T, dtype=F32), lines,
            one, square, one, square, vmem(4, T, dtype=F32), vmem(N, 4, T, dtype=F32), square,
            twos, twos, fours, fours, square, square, tall, tall,
            wide, wide, wide, wide, vmem(2, T, SEQ), vmem(2, HALF, T, dtype=F32), vmem(2, 2 * T, T, dtype=F32),
            vmem(T, N * T, dtype=F32),
            vmem(6, T, T), pltpu.SemaphoreType.DMA((15,)), pltpu.SemaphoreType.DMA((15,)), pltpu.SemaphoreType.DMA((10,)),
            pltpu.SemaphoreType.REGULAR, pltpu.SemaphoreType.DMA((6,)),
        ],
        compiler_params=pltpu.CompilerParams(
            collective_id=0, has_side_effects=True, vmem_limit_bytes=60 * 1024 * 1024
        ),
        name="pair_backward",
    )(order.reshape(1, -1), queries, keys_in, values, hq, hv, taps, gain.reshape(1, -1), upstream)
    return pl.pallas_call(
        unpack,
        out_shape=(jax.ShapeDtypeStruct((T, T), BF16),) * 6,
        in_specs=[pl.BlockSpec(memory_space=pltpu.VMEM)],
        out_specs=(pl.BlockSpec(memory_space=pltpu.VMEM),) * 6,
        name="unpack",
    )(packed)


def solution(mesh):
    rows = P("ctx", "ch")
    return jax.shard_map(
        per_device,
        mesh=mesh,
        in_specs=(rows,) * 6 + (P("ch"), rows, P()),
        out_specs=(rows,) * 6,
        check_vma=False,
    )
```
